256 devices in a mesh: group: 32 (over z, x), seq: 8 (over y, core).
Axes of the slice: x: 4, y: 4, z: 8, core: 2. Of those that a mesh axis runs over, the one named last changes fastest.
Arguments:
- rollouts: bfloat16 [32768, 4096], P(('group', 'seq')), may hold values from -40 to 40
- plan: int32 [256, 128], P('group'), may hold values from 0 to 127, each once within a row
- lengths: int32 [32, 4], P('group'), may hold values from 1 to 512, 1024 in all within a row
- rewards: float32 [32, 4], P('group'), may hold values from -4 to 4
- output_gradient: bfloat16 [32768, 4096], P('group', 'seq'), may hold values from -0.078125 to 0.078125
- query_projection: bfloat16 [4096, 4096], P(None, 'seq'), may hold values from -1 to 1
- key_projection: bfloat16 [4096, 512], P('group'), may hold values from -1 to 1
- value_projection: bfloat16 [4096, 512], P('group'), may hold values from -0.09375 to 0.09375
- adapter_down_query: bfloat16 [4096, 32], replicated, may hold values from -0.09375 to 0.09375
- adapter_up_query: bfloat16 [32, 4096], P(None, 'seq'), may hold values from -1 to 1
- adapter_down_value: bfloat16 [4096, 32], replicated, may hold values from -0.09375 to 0.09375
- adapter_up_value: bfloat16 [32, 512], replicated, may hold values from -1 to 1
Outputs:
- grad_a_query: float32 [4096, 32], replicated
- grad_a_value: float32 [4096, 32], replicated
- grad_b_query: float32 [32, 4096], replicated
- grad_b_value: float32 [32, 512], replicated
The draws below stay inside these ranges and needn't reach their ends.
Inputs may be any that keep to these rules, and one draw needn't show every extreme that they name: Each row of plan is a permutation of 0 .. 127. Each group's lengths sum to 1024.
All inputs are finite; a program needn't handle non-finite values.
Results may differ from the reference program's by a relative error of at most 0.013.
The reference program's roundings to bfloat16 on the way count: a program that leaves them out, or rounds other values in their place, can miss the bound.
Values may be sent and summed in bfloat16 or wider, within the bound.
No kernel may reach another device: no remote copies, remote signals or barrier semaphores. Data moves between devices by JAX's collectives and lax.ppermute only.
A program may use at most 128 MiB of HBM per device.

```python
import math
import jax
import jax.numpy as jnp
import numpy as np
from jax import lax

MODEL_WIDTH = 4096
QUERY_HEADS = 32
KEY_VALUE_HEADS = 4
HEAD_WIDTH = 128
ADAPTER_RANK = 32
NSEG = 4
TOK_DEV = 128
TOK_GRP = 1024
TOKENS = 32768
N_GROUP = 32
N_SEQ = 8


def draw_query_projection(key, part):
    key = jax.random.fold_in(key, 1)
    new_random_key = jnp.clip(jax.random.normal(key, (MODEL_WIDTH, QUERY_HEADS * HEAD_WIDTH), jnp.float32), -4.0, 4.0) * MODEL_WIDTH ** (-0.5)
    return new_random_key.astype(jnp.bfloat16)


def draw_key_projection(key, part):
    key = jax.random.fold_in(key, 2)
    new_random_key = jnp.clip(jax.random.normal(key, (MODEL_WIDTH, KEY_VALUE_HEADS * HEAD_WIDTH), jnp.float32), -4.0, 4.0) * MODEL_WIDTH ** (-0.5)
    return new_random_key.astype(jnp.bfloat16)


def draw_rollouts(key, part):
    key = jax.random.fold_in(key, 3)
    subkeys = jax.random.split(key, 1)
    base = jnp.clip(jax.random.normal(subkeys[0], (TOKENS, MODEL_WIDTH), jnp.float32), -6.0, 6.0)
    return base.astype(jnp.bfloat16)


def block_levels(own_key, extent, cuts, smallest, top_value):
    level, own = 1.0, jax.random.fold_in(own_key, 6)
    for dim, parts in cuts:
        steps = jnp.exp(jax.random.uniform(jax.random.fold_in(own, dim), (parts,), jnp.float32, smallest / len(cuts), top_value / len(cuts)))
        level = level * jnp.repeat(steps, extent[dim] // parts).reshape([-1 if axis == dim else 1 for axis in range(len(extent))])
    return level


def profile(number_of, total, limit, skew):
    weights = [(1 << 20) // math.isqrt(grade ** skew) + 1 for grade in range(2, number_of + 1)]
    surplus, holding = total - limit - (number_of - 1), [1] * (number_of - 1)
    while surplus > 0:
        movable = [i for i in range(number_of - 1) if holding[i] < limit]
        pool, budget = sum([weights[i] for i in movable]), surplus
        for i in movable:
            addition = min(limit - holding[i], max(1, budget * weights[i] // pool), surplus)
            holding[i] = holding[i] + addition
            surplus = surplus - addition
    return np.array([limit] + holding)


def ragged(key, amount, total, bound, slope):
    if amount == 2:
        one = jax.random.randint(key, (), max(1, total - bound), min(bound, total - 1) + 1)
        return jnp.stack([one, total - one])
    sizes = jnp.asarray(profile(amount, total, bound, slope), jnp.int32)
    couples = (amount - 1) // 2
    donor, sink = sizes[1:1 + 2 * couples:2], sizes[2:2 + 2 * couples:2]
    slack = jnp.minimum(donor - 1, bound - sink)
    shifted = jax.random.randint(jax.random.fold_in(key, 1), (couples,), 0, 1 << 20) % (slack + 1)
    sizes = sizes.at[1:1 + 2 * couples:2].set(donor - shifted).at[2:2 + 2 * couples:2].set(sink + shifted)
    return sizes[jax.random.permutation(jax.random.fold_in(key, 2), amount)]


def noise(stream_key, dims, width, bound, cuts=(), kind=jnp.bfloat16):
    result = width * jax.random.normal(stream_key, dims, jnp.float32)
    if cuts:
        result = result * block_levels(stream_key, dims, cuts, -0.22, 0.18)
    return jnp.clip(result, -bound, bound).astype(kind)


def setup_inputs(seed: int = 0) -> dict:
    seeds = jax.random.split(jax.random.key(seed), 13)
    rollouts = draw_rollouts(jax.random.fold_in(seeds[12], 71), 0)
    plan = jax.vmap(lambda own: jax.random.permutation(own, TOK_DEV))(jax.random.split(seeds[1], (N_GROUP * N_SEQ))).reshape((N_GROUP * N_SEQ, TOK_DEV)).astype(jnp.int32)
    lengths = jax.vmap(lambda own: ragged(own, NSEG, TOK_GRP, TOK_GRP // 2, 2))(jax.random.split(seeds[2], N_GROUP)).reshape((N_GROUP, NSEG)).astype(jnp.int32)
    rewards = noise(seeds[3], (N_GROUP, NSEG), 1.0, 4.0, ((0, 32),), jnp.float32)
    output_gradient = noise(seeds[4], (TOKENS, QUERY_HEADS * HEAD_WIDTH), (TOKENS ** -0.5), 0.078125, ((0, 32), (1, 8)))
    query_projection = draw_query_projection(jax.random.fold_in(seeds[12], 71), 0)
    key_projection = draw_key_projection(jax.random.fold_in(seeds[12], 71), 0)
    value_projection = noise(seeds[7], (MODEL_WIDTH, KEY_VALUE_HEADS * HEAD_WIDTH), MODEL_WIDTH ** -0.5, 0.09375, ((0, 32),))
    adapter_down_query = noise(seeds[8], (MODEL_WIDTH, ADAPTER_RANK), MODEL_WIDTH ** -0.5, 0.09375)
    adapter_up_query = noise(seeds[9], (ADAPTER_RANK, QUERY_HEADS * HEAD_WIDTH), ADAPTER_RANK ** -0.5, 1.0, ((1, 8),))
    adapter_down_value = noise(seeds[10], (MODEL_WIDTH, ADAPTER_RANK), MODEL_WIDTH ** -0.5, 0.09375)
    adapter_up_value = noise(seeds[11], (ADAPTER_RANK, KEY_VALUE_HEADS * HEAD_WIDTH), ADAPTER_RANK ** -0.5, 1.0)
    return dict(rollouts=rollouts, plan=plan, lengths=lengths, rewards=rewards, output_gradient=output_gradient, query_projection=query_projection, key_projection=key_projection, value_projection=value_projection, adapter_down_query=adapter_down_query, adapter_up_query=adapter_up_query, adapter_down_value=adapter_down_value, adapter_up_value=adapter_up_value)


rope_base = 500000.0
adapter_scale = 2.0


def pair_swap(values):
    column = lax.broadcasted_iota(jnp.int32, values.shape, 1)
    return jnp.where(column % 2 == 0, jnp.roll(values, -1, axis=1), jnp.roll(values, 1, axis=1))


def rotary(values, positions, dim_offset, head_width, sign):
    column = lax.broadcasted_iota(jnp.int32, values.shape, 1) + dim_offset
    pair_index = (column % head_width) // 2
    inv_freq = jnp.exp(pair_index.astype(jnp.float32) * (-2.0 * math.log(rope_base) / head_width))
    angles = positions[:, None].astype(jnp.float32) * inv_freq
    parity = jnp.where(column % 2 == 0, jnp.float32(-1.0), jnp.float32(1.0))
    return values * jnp.cos(angles) + sign * parity * jnp.sin(angles) * pair_swap(values)


def segment_layout(doc_lengths, total):
    doc_ends = jnp.cumsum(doc_lengths).astype(jnp.int32)
    starts = (doc_ends - doc_lengths).astype(jnp.int32)
    places = jnp.arange(total, dtype=jnp.int32)
    segment = jnp.sum((places[:, None] >= doc_ends[None, :]).astype(jnp.int32), axis=1).astype(jnp.int32)
    doc_onehot = segment[:, None] == jnp.arange(doc_lengths.shape[0], dtype=jnp.int32)[None, :]
    doc_start = jnp.sum(jnp.where(doc_onehot, starts[None, :], 0), axis=1).astype(jnp.int32)
    allowed = (segment[:, None] == segment[None, :]) & (places[:, None] >= places[None, :])
    return (places - doc_start).astype(jnp.int32), doc_onehot, allowed


def head_attention(query_head, key_head, value_head, cot_head, allowed, score_scale):
    scores = jnp.dot(query_head, key_head.T, preferred_element_type=jnp.float32) * score_scale
    scores = jnp.where(allowed, scores, -1e30)
    row_max = jnp.max(scores, axis=1, keepdims=True)
    weights = jnp.exp(scores - row_max)
    attend = weights / jnp.sum(weights, axis=1, keepdims=True)
    attend_low = attend.astype(jnp.bfloat16)
    output = jnp.dot(attend_low, value_head, preferred_element_type=jnp.float32)
    row_dot = jnp.sum(cot_head.astype(jnp.float32) * output, axis=1, keepdims=True)
    dattend = jnp.dot(cot_head, value_head.T, preferred_element_type=jnp.float32)
    dscores = (attend * (dattend - row_dot) * score_scale).astype(jnp.bfloat16)
    query_gradient = jnp.dot(dscores, key_head, preferred_element_type=jnp.float32)
    value_gradient = jnp.dot(attend_low.T, cot_head, preferred_element_type=jnp.float32)
    return query_gradient, value_gradient


def reference(rollouts, plan, lengths, rewards, output_gradient, query_projection, key_projection, value_projection, adapter_down_query, adapter_up_query, adapter_down_value, adapter_up_value):
    piece_rows = TOK_DEV // N_GROUP
    regrouped = rollouts.reshape(N_GROUP, N_SEQ, N_GROUP, piece_rows, MODEL_WIDTH).transpose(2, 1, 0, 3, 4)
    regrouped = regrouped.reshape(N_GROUP * N_SEQ, TOK_DEV, MODEL_WIDTH)
    trainer = jnp.take_along_axis(regrouped, plan.astype(jnp.int32)[:, :, None], axis=1).reshape(N_GROUP, TOK_GRP, MODEL_WIDTH)
    cotangents = output_gradient.reshape(N_GROUP, TOK_GRP, QUERY_HEADS * HEAD_WIDTH)
    heads_local_count = QUERY_HEADS // N_SEQ
    key_value_sharing = N_SEQ // KEY_VALUE_HEADS
    score_scale = HEAD_WIDTH ** -0.5

    def one_group(group_items):
        hidden_state, doc_lengths, doc_reward, cotangent = group_items
        positions, doc_onehot, allowed = segment_layout(doc_lengths, TOK_GRP)
        advantage = doc_reward - jnp.mean(doc_reward)
        adv_rows = jnp.sum(jnp.where(doc_onehot, advantage[None, :], 0.0), axis=1)
        cot_low = (cotangent.astype(jnp.float32) * adv_rows[:, None]).astype(jnp.bfloat16)
        query_reduced = jnp.dot(hidden_state, adapter_down_query, preferred_element_type=jnp.float32).astype(jnp.bfloat16)
        value_reduced = jnp.dot(hidden_state, adapter_down_value, preferred_element_type=jnp.float32).astype(jnp.bfloat16)
        query_complete = jnp.dot(hidden_state, query_projection, preferred_element_type=jnp.float32) + adapter_scale * jnp.dot(query_reduced, adapter_up_query, preferred_element_type=jnp.float32)
        query_all = rotary(query_complete, positions, 0, HEAD_WIDTH, 1.0).astype(jnp.bfloat16)
        key_all = rotary(jnp.dot(hidden_state, key_projection, preferred_element_type=jnp.float32), positions, 0, HEAD_WIDTH, 1.0).astype(jnp.bfloat16)
        value_complete = jnp.dot(hidden_state, value_projection, preferred_element_type=jnp.float32) + adapter_scale * jnp.dot(value_reduced, adapter_up_value, preferred_element_type=jnp.float32)
        value_all = value_complete.astype(jnp.bfloat16)

        def one_block(block):
            column_offset = (block * heads_local_count * HEAD_WIDTH).astype(jnp.int32)
            key_value_offset = ((block // key_value_sharing) * HEAD_WIDTH).astype(jnp.int32)
            query_block = lax.dynamic_slice_in_dim(query_all, column_offset, heads_local_count * HEAD_WIDTH, 1)
            cot_block = lax.dynamic_slice_in_dim(cot_low, column_offset, heads_local_count * HEAD_WIDTH, 1)
            key_head = lax.dynamic_slice_in_dim(key_all, key_value_offset, HEAD_WIDTH, 1)
            value_head = lax.dynamic_slice_in_dim(value_all, key_value_offset, HEAD_WIDTH, 1)
            query_lifted = lax.dynamic_slice_in_dim(adapter_up_query, column_offset, heads_local_count * HEAD_WIDTH, 1)
            value_lifted = lax.dynamic_slice_in_dim(adapter_up_value, key_value_offset, HEAD_WIDTH, 1)
            query_heads = query_block.reshape(TOK_GRP, heads_local_count, HEAD_WIDTH).transpose(1, 0, 2)
            cot_heads = cot_block.reshape(TOK_GRP, heads_local_count, HEAD_WIDTH).transpose(1, 0, 2)

            def per_head(pair_items):
                return head_attention(pair_items[0], key_head, value_head, pair_items[1], allowed, score_scale)

            query_grads, value_grads = lax.map(per_head, (query_heads, cot_heads))
            value_gradient = jnp.sum(value_grads, axis=0).astype(jnp.bfloat16)
            query_flat = query_grads.transpose(1, 0, 2).reshape(TOK_GRP, heads_local_count * HEAD_WIDTH)
            query_gradient = rotary(query_flat, positions, 0, HEAD_WIDTH, -1.0).astype(jnp.bfloat16)
            query_backward = jnp.dot(query_gradient, query_lifted.T, preferred_element_type=jnp.float32).astype(jnp.bfloat16)
            value_backward = jnp.dot(value_gradient, value_lifted.T, preferred_element_type=jnp.float32).astype(jnp.bfloat16)
            query_down_gradient = adapter_scale * jnp.dot(hidden_state.T, query_backward, preferred_element_type=jnp.float32)
            value_down_gradient = adapter_scale * jnp.dot(hidden_state.T, value_backward, preferred_element_type=jnp.float32)
            query_up_gradient = adapter_scale * jnp.dot(query_reduced.T, query_gradient, preferred_element_type=jnp.float32)
            value_up_gradient = adapter_scale * jnp.dot(value_reduced.T, value_gradient, preferred_element_type=jnp.float32)
            return query_down_gradient, value_down_gradient, query_up_gradient, value_up_gradient

        block_pieces_list = lax.map(one_block, jnp.arange(N_SEQ, dtype=jnp.int32))
        query_down_gradient = jnp.sum(block_pieces_list[0], axis=0)
        value_down_gradient = jnp.sum(block_pieces_list[1], axis=0)
        query_up_gradient = block_pieces_list[2].transpose(1, 0, 2).reshape(ADAPTER_RANK, QUERY_HEADS * HEAD_WIDTH)
        value_up_gradient = jnp.sum(block_pieces_list[3].reshape(KEY_VALUE_HEADS, key_value_sharing, ADAPTER_RANK, HEAD_WIDTH), axis=1).transpose(1, 0, 2).reshape(ADAPTER_RANK, KEY_VALUE_HEADS * HEAD_WIDTH)
        return query_down_gradient, value_down_gradient, query_up_gradient, value_up_gradient

    partials = lax.map(one_group, (trainer, lengths, rewards, cotangents))
    return (jnp.sum(partials[0], axis=0), jnp.sum(partials[1], axis=0), jnp.sum(partials[2], axis=0), jnp.sum(partials[3], axis=0))
```

```python
import functools
import math

import jax
import jax.numpy as jnp
from jax import lax
from jax.experimental import pallas as pl
from jax.experimental.pallas import tpu as pltpu
from jax.sharding import Mesh
from jax.sharding import PartitionSpec as P

HEAD = 128
KV_HEADS = 4
RANK = 32
ROPE_BASE = 500000.0
ADAPTER_SCALE = 2.0
LOG2E = math.log2(math.e)
BF = jnp.bfloat16
F32 = jnp.float32
MIB = 1 << 20


def mm(a, b, ca=1, cb=0):
    return lax.dot_general(a, b, (((ca,), (cb,)), ((), ())), preferred_element_type=F32)


def rope(u, cos, ssin, sign):
    even = lax.broadcasted_iota(jnp.int32, u.shape, 1) % 2 == 0
    swapped = jnp.where(even, pltpu.roll(u, HEAD - 1, 1), pltpu.roll(u, 1, 1))
    if sign > 0:
        return u * cos + ssin * swapped
    return u * cos - ssin * swapped


def params(mib):
    return pltpu.CompilerParams(vmem_limit_bytes=mib * MIB)


def q_kernel(idx, al, ar, bl, br, wq, wl, upq, cos_a, sin_a, cos_b, sin_b, q_out, low_out, accq, accl):
    step, steps = pl.program_id(0), pl.num_programs(0)

    @pl.when(step == 0)
    def _():
        accq[...] = jnp.zeros_like(accq)
        accl[...] = jnp.zeros_like(accl)

    def add(a, b):
        h = jnp.concatenate([a[...], b[...]], axis=0)
        accq[...] += mm(h, wq[...])
        accl[...] += mm(h, wl[...])

    pl.when(step < steps // 2)(lambda: add(al, bl))
    pl.when(step >= steps // 2)(lambda: add(ar, br))

    @pl.when(step == steps - 1)
    def _():
        low = accl[...].astype(BF)
        low_out[...] = low
        q = accq[...] + ADAPTER_SCALE * mm(low[:, :RANK], upq[...])
        cos = jnp.concatenate([cos_a[...], cos_b[...]], axis=0)
        ssin = jnp.concatenate([sin_a[...], sin_b[...]], axis=0)
        for h in range(q.shape[1] // HEAD):
            cols = slice(h * HEAD, (h + 1) * HEAD)
            q_out[:, cols] = rope(q[:, cols], cos, ssin, 1).astype(BF)


def project_q(ia, ib, al, ar, bl, br, wq, wl, upq, cos, ssin):
    rows, half = al.shape
    kb = 512
    per = half // kb
    n = wq.shape[1]
    left = lambda k, i: (0, jnp.minimum(k, per - 1))
    right = lambda k, i: (0, jnp.maximum(k - per, 0))
    spec = pl.BlockSpec
    return pl.pallas_call(
        q_kernel,
        grid_spec=pltpu.PrefetchScalarGridSpec(
            num_scalar_prefetch=1,
            grid=(2 * per,),
            in_specs=[
                spec((rows, kb), left),
                spec((rows, kb), right),
                spec((rows, kb), left),
                spec((rows, kb), right),
                spec((kb, n), lambda k, i: (k, 0)),
                spec((kb, wl.shape[1]), lambda k, i: (k, 0)),
                spec(upq.shape, lambda k, i: (0, 0)),
                spec((rows, HEAD), lambda k, i: (i[0], 0)),
                spec((rows, HEAD), lambda k, i: (i[0], 0)),
                spec((rows, HEAD), lambda k, i: (i[1], 0)),
                spec((rows, HEAD), lambda k, i: (i[1], 0)),
            ],
            out_specs=[
                spec((2 * rows, n), lambda k, i: (0, 0)),
                spec((2 * rows, wl.shape[1]), lambda k, i: (0, 0)),
            ],
            scratch_shapes=[pltpu.VMEM((2 * rows, n), F32), pltpu.VMEM((2 * rows, wl.shape[1]), F32)],
        ),
        out_shape=[
            jax.ShapeDtypeStruct((2 * rows, n), BF),
            jax.ShapeDtypeStruct((2 * rows, wl.shape[1]), BF),
        ],
        compiler_params=params(20),
        cost_estimate=pl.CostEstimate(
            flops=2 * 2 * rows * 2 * half * (n + 256), bytes_accessed=8 * MIB, transcendentals=0
        ),
        name="project_q",
    )(jnp.stack([ia, ib]), al, ar, bl, br, wq, wl, upq, cos, ssin, cos, ssin)


def kv_kernel(idx, *refs):
    hs, (wa, wb, lows, upv, cos, ssin, k_out, v_out, acc) = refs[:16], (
        refs[16],
        refs[17],
        refs[18:22],
        *refs[22:],
    )
    step, steps = pl.program_id(0), pl.num_programs(0)

    @pl.when(step == 0)
    def _():
        acc[...] = jnp.zeros_like(acc)

    def add(side):
        w = jnp.concatenate([wa[...], wb[...]], axis=1)
        for p in range(4):
            h = jnp.concatenate([hs[4 * p + side][...], hs[4 * p + 2 + side][...]], axis=0)
            acc[p] += mm(h, w)

    pl.when(step < steps // 2)(lambda: add(0))
    pl.when(step >= steps // 2)(lambda: add(1))

    @pl.when(step == steps - 1)
    def _():
        first = idx[8] == 0
        rows = acc.shape[1] // 2
        for p in range(4):
            both = acc[p]
            k = jnp.where(first, both[:, :HEAD], both[:, HEAD:])
            v = jnp.where(first, both[:, HEAD:], both[:, :HEAD])
            v = v + ADAPTER_SCALE * mm(lows[p][:, RANK:], upv[...])
            for j in range(2):
                at = pl.ds(pl.multiple_of(idx[2 * p + j] * rows, rows), rows)
                part = slice(j * rows, (j + 1) * rows)
                k_out[at, :] = rope(k[part], cos[at, :], ssin[at, :], 1).astype(BF)
                v_out[at, :] = v[part].astype(BF)


def project_kv(idx, blocks, wa, wb, lows, upv, cos, ssin):
    rows, half = blocks[0].shape
    kb = 512
    per = half // kb
    total = 8 * rows
    left = lambda k, i: (0, jnp.minimum(k, per - 1))
    right = lambda k, i: (0, jnp.maximum(k - per, 0))
    spec = pl.BlockSpec
    whole = lambda x: spec(x.shape, lambda k, i: (0, 0))
    return pl.pallas_call(
        kv_kernel,
        grid_spec=pltpu.PrefetchScalarGridSpec(
            num_scalar_prefetch=1,
            grid=(2 * per,),
            in_specs=[spec((rows, kb), left if b % 2 == 0 else right) for b in range(16)]
            + [spec((kb, HEAD), lambda k, i: (k, 0))] * 2
            + [whole(x) for x in lows]
            + [whole(upv), whole(cos), whole(ssin)],
            out_specs=[spec((total, HEAD), lambda k, i: (0, 0))] * 2,
            scratch_shapes=[pltpu.VMEM((4, 2 * rows, 2 * HEAD), F32)],
        ),
        out_shape=[jax.ShapeDtypeStruct((total, HEAD), BF)] * 2,
        compiler_params=params(20),
        cost_estimate=pl.CostEstimate(
            flops=2 * total * 2 * half * 256, bytes_accessed=10 * MIB, transcendentals=0
        ),
        name="project_kv",
    )(idx, *blocks, wa, wb, *lows, upv, cos, ssin)


def attn_kernel(idx, lens, *refs):
    qs, lows = refs[:4], refs[4:8]
    k_ref, v_ref, cot_ref, cos, ssin, upq, upv = refs[8:15]
    back_out, gbq_out, gbv_out = refs[15:18]
    q_s, low_s, qg_s, dv_s = refs[18:]
    total, width = q_s.shape
    rows = total // 8
    for p in range(4):
        for j in range(2):
            at = pl.ds(pl.multiple_of(idx[2 * p + j] * rows, rows), rows)
            q_s[at, :] = qs[p][j * rows : (j + 1) * rows, :]
            low_s[at, :] = lows[p][j * rows : (j + 1) * rows, :]
    dv_s[...] = jnp.zeros_like(dv_s)
    scale = HEAD**-0.5
    blk = 2 * rows
    longest = 512

    ends = []
    end = jnp.int32(0)
    for n in range(lens.shape[1]):
        end = end + lens[0, n]
        ends.append(end)

    def head(h, carry):
        cols = pl.ds(pl.multiple_of(h * HEAD, HEAD), HEAD)
        for r in range(total // blk):
            lo, hi = max(0, r * blk - longest), (r + 1) * blk
            at = slice(r * blk, hi)
            keys = k_ref[lo:hi, :]
            values = v_ref[lo:hi, :]
            cot = cot_ref[at, cols]
            row = lax.broadcasted_iota(jnp.int32, (blk, 1), 0) + r * blk
            start = jnp.zeros((blk, 1), jnp.int32)
            for end in ends[:-1]:
                start = jnp.where(row >= end, end, start)
            col = lax.broadcasted_iota(jnp.int32, (blk, hi - lo), 1) + lo
            allowed = (col >= start) & (col <= row)
            s = mm(q_s[at, cols], keys, 1, 1) * (scale * LOG2E)
            s = jnp.where(allowed, s, -1e30)
            w = jnp.exp2(s - jnp.max(s, axis=1, keepdims=True))
            probs = w * (1.0 / jnp.sum(w, axis=1, keepdims=True))
            low = probs.astype(BF)
            dp = mm(cot, values, 1, 1)
            rowdot = jnp.sum(low.astype(F32) * dp, axis=1, keepdims=True)
            ds = (probs * (dp - rowdot) * scale).astype(BF)
            qg_s[at, cols] = rope(mm(ds, keys), cos[at, :], ssin[at, :], -1).astype(BF)
            dv_s[lo:hi, :] += mm(low, cot, 0, 0)
        return carry

    lax.fori_loop(0, width // HEAD, head, 0)
    qg = qg_s[...]
    vg = dv_s[...].astype(BF)
    low = low_s[...]
    back_out[:RANK, :] = mm(upq[...], qg, 1, 1).astype(BF)
    back_out[RANK:, :] = mm(upv[...], vg, 1, 1).astype(BF)
    gbq_out[...] = ADAPTER_SCALE * mm(low[:, :RANK], qg, 0, 0)
    gbv = ADAPTER_SCALE * mm(low[:, RANK:], vg, 0, 0)
    for i in range(4):
        gbv_out[:, i * HEAD : (i + 1) * HEAD] = gbv[8 * i : 8 * (i + 1), :]


def attention(idx, lengths, qs, lows, k, v, cot, cos, ssin, upq, upv):
    total, width = cot.shape
    vm = pl.BlockSpec(memory_space=pltpu.VMEM)
    sm = pl.BlockSpec(memory_space=pltpu.SMEM)
    return pl.pallas_call(
        attn_kernel,
        in_specs=[sm, sm] + [vm] * 15,
        out_specs=[vm] * 3,
        out_shape=[
            jax.ShapeDtypeStruct((2 * RANK, total), BF),
            jax.ShapeDtypeStruct((RANK, width), F32),
            jax.ShapeDtypeStruct((RANK // 4, 4 * HEAD), F32),
        ],
        scratch_shapes=[
            pltpu.VMEM((total, width), BF),
            pltpu.VMEM((total, 2 * RANK), BF),
            pltpu.VMEM((total, width), BF),
            pltpu.VMEM((total, HEAD), F32),
        ],
        compiler_params=params(32),
        cost_estimate=pl.CostEstimate(flops=10**10, bytes_accessed=4 * MIB, transcendentals=4 * 10**6),
        name="attention",
    )(idx, lengths, *qs, *lows, k, v, cot, cos, ssin, upq, upv)


def down_kernel(info, back, *refs):
    hs, out = refs[:16], refs[16]
    rows = back.shape[1] // 8
    slot = info[8 + pl.program_id(0)]

    def grad(side):
        acc = None
        for p in range(4):
            parts = [
                back[:, pl.ds(pl.multiple_of(info[2 * p + j] * rows, rows), rows)] for j in range(2)
            ]
            b = jnp.concatenate(parts, axis=1)
            h = jnp.concatenate([hs[4 * p + side][...], hs[4 * p + 2 + side][...]], axis=0)
            part = mm(b, h)
            acc = part if acc is None else acc + part
        out[0] = ADAPTER_SCALE * acc

    pl.when(slot < 4)(lambda: grad(0))
    pl.when(slot >= 4)(lambda: grad(1))


def down_grads(idx, slots, back, blocks):
    rows, half = blocks[0].shape
    width = half // 4
    spec = pl.BlockSpec
    left = lambda k, i: (0, jnp.minimum(i[8 + k], 3))
    right = lambda k, i: (0, jnp.maximum(i[8 + k] - 4, 0))
    return pl.pallas_call(
        down_kernel,
        grid_spec=pltpu.PrefetchScalarGridSpec(
            num_scalar_prefetch=1,
            grid=(8,),
            in_specs=[spec(back.shape, lambda k, i: (0, 0))]
            + [spec((rows, width), left if b % 2 == 0 else right) for b in range(16)],
            out_specs=spec((1, 2 * RANK, width), lambda k, i: (k, 0, 0)),
        ),
        out_shape=jax.ShapeDtypeStruct((8, 2 * RANK, width), F32),
        compiler_params=params(20),
        cost_estimate=pl.CostEstimate(
            flops=2 * 8 * rows * 2 * half * 256, bytes_accessed=10 * MIB, transcendentals=0
        ),
        name="down_grads",
    )(jnp.concatenate([idx[:8], slots]), back, *blocks)


def pack_kernel(slot, a0, a1, a2, a3, gbq, v0, v1, out):
    n = out.shape[0]
    down = a0[...] + a1[...] + a2[...] + a3[...]
    gbv = v0[...] + v1[...]
    wide = out.shape[2]
    for i in range(n):
        for j in range(n):

            @pl.when(slot[i] == j)
            def _():
                cols = slice(j * wide, (j + 1) * wide)
                out[i, : 2 * RANK, :] = down[:, cols]
                out[i, 2 * RANK : 3 * RANK, :] = gbq[:, cols]
                out[i, 3 * RANK :, :] = gbv[:, cols]


def pack(slot, pieces, gbq, v0, v1):
    n = slot.shape[0]
    vm = pl.BlockSpec(memory_space=pltpu.VMEM)
    sm = pl.BlockSpec(memory_space=pltpu.SMEM)
    return pl.pallas_call(
        pack_kernel,
        in_specs=[sm] + [vm] * 7,
        out_specs=vm,
        out_shape=jax.ShapeDtypeStruct((n, 3 * RANK + 8, gbq.shape[1] // n), F32),
        compiler_params=params(16),
        name="pack",
    )(slot, *pieces, gbq, v0, v1)


def unpack_kernel(n, info, *refs):
    ins, (gaq, gav, gbq, gbv) = refs[: 8 * n], refs[8 * n :]
    for b in range(8):
        seq = info[b]
        for i in range(n):
            ref = ins[b * n + i]
            wide = ref.shape[1]
            col = pl.multiple_of(seq * (n * wide) + info[8 + i] * wide, wide)
            gaq[pl.ds(col, wide), :] = ref[:RANK, :].T
            gav[pl.ds(col, wide), :] = ref[RANK : 2 * RANK, :].T
            gbq[:, pl.ds(col, wide)] = ref[2 * RANK : 3 * RANK, :]
            if b % 2 == 0:
                at = pl.ds(pl.multiple_of((seq // 2) * HEAD, HEAD), HEAD)
                for j in range(wide // HEAD):
                    first = (info[8 + i] * (wide // HEAD) + j) * 8
                    part = pl.ds(pl.multiple_of(first, 8), 8)
                    gbv[part, at] = ref[3 * RANK :, j * HEAD : (j + 1) * HEAD]


def unpack(info, pieces, n, model):
    vm = pl.BlockSpec(memory_space=pltpu.VMEM)
    sm = pl.BlockSpec(memory_space=pltpu.SMEM)
    return pl.pallas_call(
        functools.partial(unpack_kernel, n),
        in_specs=[sm] + [vm] * (8 * n),
        out_specs=[vm] * 4,
        out_shape=[
            jax.ShapeDtypeStruct((model, RANK), F32),
            jax.ShapeDtypeStruct((model, RANK), F32),
            jax.ShapeDtypeStruct((RANK, model), F32),
            jax.ShapeDtypeStruct((RANK, KV_HEADS * HEAD), F32),
        ],
        compiler_params=params(24),
        name="unpack",
    )(info, *pieces)


def shift(value, axis, by):
    n = lax.axis_size(axis)
    return lax.ppermute(value, axis, [(i, (i + by) % n) for i in range(n)])


def shards(
    rollouts,
    plan,
    lengths,
    rewards,
    output_gradient,
    query_projection,
    key_projection,
    value_projection,
    adapter_down_query,
    adapter_up_query,
    adapter_down_value,
    adapter_up_value,
):
    nz, nx = lax.axis_size("z"), lax.axis_size("x")
    x, y, core = lax.axis_index("x"), lax.axis_index("y"), lax.axis_index("core")
    seq = 2 * y + core
    total, width = output_gradient.shape
    model = rollouts.shape[1]
    half = model // 2
    swap = lambda v: lax.ppermute(v, "core", [(0, 1), (1, 0)])

    ys = [(y + d) % 4 for d in (0, 3, 1, 2)]
    idx = jnp.stack([2 * a + b for a in ys for b in (core, 1 - core)] + [core]).astype(jnp.int32)

    arrived = lax.all_to_all(rollouts, ("z", "x"), split_axis=0, concat_axis=0, tiled=True)
    order = lax.dynamic_index_in_dim(plan, seq, 0, keepdims=False)
    own_l = arrived[:, :half].at[order].get(mode="promise_in_bounds")
    own_r = arrived[:, half:].at[order].get(mode="promise_in_bounds")

    take = lambda w: lax.dynamic_slice_in_dim(w, y * HEAD, HEAD, 1)
    mine = jnp.where(core == 0, take(key_projection), take(value_projection))
    wa = lax.all_gather(mine, ("z", "x"), axis=0, tiled=True)
    wb = swap(wa)
    up_value = take(adapter_up_value)
    down_both = jnp.concatenate([adapter_down_query, adapter_down_value], axis=1)

    ends = jnp.cumsum(lengths[0])
    starts = ends - lengths[0]
    places = jnp.arange(total, dtype=jnp.int32)
    segment = jnp.sum((places[:, None] >= ends[None, :]).astype(jnp.int32), axis=1)
    onehot = segment[:, None] == jnp.arange(lengths.shape[1], dtype=jnp.int32)[None, :]
    positions = places - jnp.sum(jnp.where(onehot, starts[None, :], 0), axis=1)
    column = jnp.arange(HEAD, dtype=jnp.int32)
    inv_freq = jnp.exp((column // 2).astype(F32) * (-2.0 * math.log(ROPE_BASE) / HEAD))
    angles = positions[:, None].astype(F32) * inv_freq[None, :]
    cos = jnp.cos(angles)
    ssin = jnp.where(column % 2 == 0, F32(-1.0), F32(1.0))[None, :] * jnp.sin(angles)
    advantage = rewards[0] - jnp.mean(rewards[0])
    adv_rows = jnp.sum(jnp.where(onehot, advantage[None, :], 0.0), axis=1)
    cot = (output_gradient.astype(F32) * adv_rows[:, None]).astype(BF)

    up_l, down_r = shift(own_l, "y", 1), shift(own_r, "y", -1)
    up_r, down_l = shift(own_r, "y", 1), shift(own_l, "y", -1)
    far_l, far_r = shift(up_l, "y", 1), shift(down_r, "y", -1)
    blocks = []
    qs, lows = [], []
    for p, (l, r) in enumerate([(own_l, own_r), (up_l, up_r), (down_l, down_r), (far_l, far_r)]):
        ol, orr = swap(l), swap(r)
        blocks += [l, r, ol, orr]
        q, low = project_q(
            idx[2 * p],
            idx[2 * p + 1],
            l,
            r,
            ol,
            orr,
            query_projection,
            down_both,
            adapter_up_query,
            cos,
            ssin,
        )
        qs.append(q)
        lows.append(low)
    k, v = project_kv(idx, blocks, wa, wb, lows, up_value, cos, ssin)
    back, gbq, gbv = attention(
        idx, lengths, qs, lows, k, v, cot, cos, ssin, adapter_up_query, up_value
    )

    slots = jnp.stack([2 * ((y + b) % 4) + c for c in (core, 1 - core) for b in range(4)])
    down = down_grads(idx, slots.astype(jnp.int32), back, blocks)
    gbv_other = swap(gbv)
    down = down[:4] + swap(down[4:])
    pieces = [down[0]] + [shift(down[b], "y", b) for b in (1, 2, 3)]
    xs = [(x + i) % nx for i in range(nx)]
    packed = pack(jnp.stack(xs).astype(jnp.int32), pieces, gbq, gbv, gbv_other)
    part = packed[0]
    for i in range(1, nx):
        part = part + shift(packed[i], "x", i)
    full = part
    for i in range(1, nz):
        full = full + shift(part, "z", i)
    by_x = [full] + [shift(full, "x", i) for i in range(1, nx)]
    from_x = [(x - i) % nx for i in range(nx)]
    mine = jnp.concatenate(by_x, axis=0)
    ups = shift(mine, "y", 1)
    downs = shift(mine, "y", -1)
    cut = mine.shape[0] // 2
    far = [shift(ups[:cut], "y", 1), shift(downs[cut:], "y", -1)]
    got = [[mine], [ups], [downs], far]
    flat = []
    size = full.shape[0]
    for group in got:
        for side in (lambda v: v, swap):
            moved = [side(v) for v in group]
            for v in moved:
                flat += [v[i : i + size] for i in range(0, v.shape[0], size)]
    info = jnp.stack([idx[b] for b in range(8)] + from_x).astype(jnp.int32)
    return tuple(unpack(info, flat, nx, model))


def solution(mesh):
    groups, _ = mesh.devices.shape
    nx = 4 if groups % 4 == 0 else groups
    grid = Mesh(mesh.devices.reshape(groups // nx, nx, 4, 2), ("z", "x", "y", "core"))
    group, seq = ("z", "x"), ("y", "core")
    in_specs = (
        P(group + seq, None),
        P(group, None),
        P(group, None),
        P(group, None),
        P(group, seq),
        P(None, seq),
        P(group, None),
        P(group, None),
        P(),
        P(None, seq),
        P(),
        P(),
    )
    return jax.shard_map(
        shards, mesh=grid, in_specs=in_specs, out_specs=(P(), P(), P(), P()), check_vma=False
    )
```

```python
import functools
import math

import jax
import jax.numpy as jnp
from jax import lax
from jax.experimental import pallas as pl
from jax.experimental.pallas import tpu as pltpu
from jax.sharding import Mesh
from jax.sharding import PartitionSpec as P

HEAD = 128
KV_HEADS = 4
RANK = 32
ROPE_BASE = 500000.0
ADAPTER_SCALE = 2.0
LOG2E = math.log2(math.e)
BF = jnp.bfloat16
F32 = jnp.float32
MIB = 1 << 20


def mm(a, b, ca=1, cb=0):
    return lax.dot_general(a, b, (((ca,), (cb,)), ((), ())), preferred_element_type=F32)


def rope(u, cos, ssin, sign):
    even = lax.broadcasted_iota(jnp.int32, u.shape, 1) % 2 == 0
    swapped = jnp.where(even, pltpu.roll(u, HEAD - 1, 1), pltpu.roll(u, 1, 1))
    if sign > 0:
        return u * cos + ssin * swapped
    return u * cos - ssin * swapped


def params(mib):
    return pltpu.CompilerParams(vmem_limit_bytes=mib * MIB)


VM = pl.BlockSpec(memory_space=pltpu.VMEM)
SM = pl.BlockSpec(memory_space=pltpu.SMEM)


def fold_kernel(piece, x, out):
    rows, half = x.shape[0], x.shape[1] // 2
    r = lax.broadcasted_iota(jnp.int32, (2 * rows, 2 * rows), 0)
    c = lax.broadcasted_iota(jnp.int32, (2 * rows, 2 * rows), 1)
    inside = r % (2 * piece)
    source = (r // (2 * piece)) * piece + inside % piece + jnp.where(inside >= piece, rows, 0)
    pick = (source == c).astype(F32).astype(BF)
    both = jnp.concatenate([x[:, :half], x[:, half:]], axis=0)
    out[...] = mm(pick, both).astype(BF)


def fold(x, piece):
    rows, model = x.shape
    return pl.pallas_call(
        functools.partial(fold_kernel, piece),
        in_specs=[VM],
        out_specs=VM,
        out_shape=jax.ShapeDtypeStruct((2 * rows, model // 2), BF),
        compiler_params=params(16),
        name="fold",
    )(x)


def order_kernel(piece, plan, x, left, right):
    rows = left.shape[0]
    want = plan[...]
    want = (want // piece) * (2 * piece) + want % piece
    r = lax.broadcasted_iota(jnp.int32, (2 * rows, rows), 0)
    pick_l = (r == want).astype(F32).astype(BF)
    pick_r = (r == want + piece).astype(F32).astype(BF)
    left[...] = mm(pick_l, x[...], 0, 0).astype(BF)
    right[...] = mm(pick_r, x[...], 0, 0).astype(BF)


def order_rows(plan, x, piece):
    rows, half = x.shape[0] // 2, x.shape[1]
    return pl.pallas_call(
        functools.partial(order_kernel, piece),
        in_specs=[VM, VM],
        out_specs=[VM, VM],
        out_shape=[jax.ShapeDtypeStruct((rows, half), BF)] * 2,
        compiler_params=params(16),
        name="order_rows",
    )(plan, x)


def weights_kernel(info, a, b, out):
    first = info[0] == 0
    n = a.shape[0] // HEAD

    def block(i, carry):
        at = pl.ds(pl.multiple_of(i * HEAD, HEAD), HEAD)
        to = pl.ds(pl.multiple_of(info[1 + i] * HEAD, HEAD), HEAD)
        one, two = a[at, :], b[at, :]
        out[to, :HEAD] = jnp.where(first, one, two)
        out[to, HEAD:] = jnp.where(first, two, one)
        return carry

    lax.fori_loop(0, n, block, 0)


def join_weights(info, a, b):
    return pl.pallas_call(
        weights_kernel,
        in_specs=[SM, VM, VM],
        out_specs=VM,
        out_shape=jax.ShapeDtypeStruct((a.shape[0], 2 * HEAD), BF),
        compiler_params=params(16),
        name="join_weights",
    )(info, a, b)


def q_kernel(pair, idx, al, ar, bl, br, wq, dt, upq, cos, ssin, q_out, low_out):
    rows, half = al.shape
    left = jnp.concatenate([al[...], bl[...]], axis=0)
    right = jnp.concatenate([ar[...], br[...]], axis=0)
    low = mm(left, dt[:, :half], 1, 1) + mm(right, dt[:, half:], 1, 1)
    low = low.astype(BF)
    low_out[...] = low
    ats = [pl.ds(pl.multiple_of(idx[2 * pair + j] * rows, rows), rows) for j in range(2)]
    c = jnp.concatenate([cos[at, :] for at in ats], axis=0)
    s = jnp.concatenate([ssin[at, :] for at in ats], axis=0)
    wide = 2 * HEAD
    for h in range(wq.shape[1] // wide):
        cols = slice(h * wide, (h + 1) * wide)
        q = mm(left, wq[:half, cols]) + mm(right, wq[half:, cols])
        q = q + ADAPTER_SCALE * mm(low[:, :RANK], upq[:, cols])
        for j in range(2):
            one = slice(h * wide + j * HEAD, h * wide + (j + 1) * HEAD)
            q_out[:, one] = rope(q[:, j * HEAD : (j + 1) * HEAD], c, s, 1).astype(BF)


def project_q(pair, idx, al, ar, bl, br, wq, dt, upq, cos, ssin):
    rows, half = al.shape
    n = wq.shape[1]
    return pl.pallas_call(
        functools.partial(q_kernel, pair),
        in_specs=[SM] + [VM] * 9,
        out_specs=[VM, VM],
        out_shape=[
            jax.ShapeDtypeStruct((2 * rows, n), BF),
            jax.ShapeDtypeStruct((2 * rows, 2 * RANK), BF),
        ],
        compiler_params=params(16),
        cost_estimate=pl.CostEstimate(
            flops=2 * 2 * rows * 2 * half * (n + 256), bytes_accessed=MIB, transcendentals=0
        ),
        name="project_q",
    )(idx, al, ar, bl, br, wq, dt, upq, cos, ssin)


def kv_kernel(idx, *refs):
    hs, w, lows, (upv, cos, ssin, k_out, v_out) = refs[:16], refs[16], refs[17:21], refs[21:]
    rows, half = hs[0].shape
    for p in range(4):
        left = jnp.concatenate([hs[4 * p][...], hs[4 * p + 2][...]], axis=0)
        right = jnp.concatenate([hs[4 * p + 1][...], hs[4 * p + 3][...]], axis=0)
        both = mm(left, w[:half, :]) + mm(right, w[half:, :])
        k = both[:, :HEAD]
        v = both[:, HEAD:] + ADAPTER_SCALE * mm(lows[p][:, RANK:], upv[...])
        for j in range(2):
            at = pl.ds(pl.multiple_of(idx[2 * p + j] * rows, rows), rows)
            part = slice(j * rows, (j + 1) * rows)
            k_out[at, :] = rope(k[part], cos[at, :], ssin[at, :], 1).astype(BF)
            v_out[at, :] = v[part].astype(BF)


def project_kv(idx, blocks, w, lows, upv, cos, ssin):
    rows, half = blocks[0].shape
    total = 8 * rows
    return pl.pallas_call(
        kv_kernel,
        in_specs=[SM] + [VM] * 24,
        out_specs=[VM, VM],
        out_shape=[jax.ShapeDtypeStruct((total, HEAD), BF)] * 2,
        compiler_params=params(16),
        cost_estimate=pl.CostEstimate(
            flops=2 * total * 2 * half * 256, bytes_accessed=MIB, transcendentals=0
        ),
        name="project_kv",
    )(idx, *blocks, w, *lows, upv, cos, ssin)


def attn_kernel(idx, lens, *refs):
    qs, lows = refs[:4], refs[4:8]
    k_ref, v_ref, cot_ref, cos, ssin, upq, upv = refs[8:15]
    back_out, gbq_out, gbv_out = refs[15:18]
    q_s, low_s, qg_s, dv_s = refs[18:]
    total, width = q_s.shape
    rows = total // 8
    for p in range(4):
        for j in range(2):
            at = pl.ds(pl.multiple_of(idx[2 * p + j] * rows, rows), rows)
            q_s[at, :] = qs[p][j * rows : (j + 1) * rows, :]
            low_s[at, :] = lows[p][j * rows : (j + 1) * rows, :]
    dv_s[...] = jnp.zeros_like(dv_s)
    scale = HEAD**-0.5
    blk = 2 * rows
    longest = 512

    ends = []
    end = jnp.int32(0)
    for n in range(lens.shape[1]):
        end = end + lens[0, n]
        ends.append(end)

    def head(h, carry):
        cols = pl.ds(pl.multiple_of(h * HEAD, HEAD), HEAD)
        for r in range(total // blk):
            lo, hi = max(0, r * blk - longest), (r + 1) * blk
            at = slice(r * blk, hi)
            keys = k_ref[lo:hi, :]
            values = v_ref[lo:hi, :]
            cot = cot_ref[at, cols]
            row = lax.broadcasted_iota(jnp.int32, (blk, 1), 0) + r * blk
            start = jnp.zeros((blk, 1), jnp.int32)
            for end in ends[:-1]:
                start = jnp.where(row >= end, end, start)
            col = lax.broadcasted_iota(jnp.int32, (blk, hi - lo), 1) + lo
            allowed = (col >= start) & (col <= row)
            s = mm(q_s[at, cols], keys, 1, 1) * (scale * LOG2E)
            s = jnp.where(allowed, s, -1e30)
            w = jnp.exp2(s - jnp.max(s, axis=1, keepdims=True))
            probs = w * (1.0 / jnp.sum(w, axis=1, keepdims=True))
            low = probs.astype(BF)
            dp = mm(cot, values, 1, 1)
            rowdot = jnp.sum(low.astype(F32) * dp, axis=1, keepdims=True)
            ds = (probs * (dp - rowdot) * scale).astype(BF)
            qg_s[at, cols] = rope(mm(ds, keys), cos[at, :], ssin[at, :], -1).astype(BF)
            dv_s[lo:hi, :] += mm(low, cot, 0, 0)
        return carry

    lax.fori_loop(0, width // HEAD, head, 0)
    qg = qg_s[...]
    vg = dv_s[...].astype(BF)
    low = low_s[...]
    back_out[:RANK, :] = mm(upq[...], qg, 1, 1).astype(BF)
    back_out[RANK:, :] = mm(upv[...], vg, 1, 1).astype(BF)
    gbq_out[...] = ADAPTER_SCALE * mm(low[:, :RANK], qg, 0, 0)
    gbv = ADAPTER_SCALE * mm(low[:, RANK:], vg, 0, 0)
    for i in range(4):
        gbv_out[:, i * HEAD : (i + 1) * HEAD] = gbv[8 * i : 8 * (i + 1), :]


def attention(idx, lengths, qs, lows, k, v, cot, cos, ssin, upq, upv):
    total, width = cot.shape
    return pl.pallas_call(
        attn_kernel,
        in_specs=[SM, SM] + [VM] * 15,
        out_specs=[VM] * 3,
        out_shape=[
            jax.ShapeDtypeStruct((2 * RANK, total), BF),
            jax.ShapeDtypeStruct((RANK, width), F32),
            jax.ShapeDtypeStruct((RANK // 4, 4 * HEAD), F32),
        ],
        scratch_shapes=[
            pltpu.VMEM((total, width), BF),
            pltpu.VMEM((total, 2 * RANK), BF),
            pltpu.VMEM((total, width), BF),
            pltpu.VMEM((total, HEAD), F32),
        ],
        compiler_params=params(32),
        cost_estimate=pl.CostEstimate(flops=10**10, bytes_accessed=4 * MIB, transcendentals=4 * 10**6),
        name="attention",
    )(idx, lengths, *qs, *lows, k, v, cot, cos, ssin, upq, upv)


def down_kernel(info, back, *refs):
    hs, out = refs[:16], refs[16]
    rows, half = hs[0].shape
    width = out.shape[2]
    parts = [back[:, pl.ds(pl.multiple_of(info[b] * rows, rows), rows)] for b in range(8)]
    lhs = jnp.concatenate(parts, axis=1)
    per = half // width
    for j in range(2 * per):
        side, cols = j // per, slice(j % per * width, (j % per + 1) * width)
        h = jnp.concatenate([hs[2 * b + side][:, cols] for b in range(8)], axis=0)
        out[info[8 + j]] = ADAPTER_SCALE * mm(lhs, h)


def down_grads(idx, slot_of, back, blocks):
    rows, half = blocks[0].shape
    width = half // 4
    return pl.pallas_call(
        down_kernel,
        in_specs=[SM] + [VM] * 17,
        out_specs=VM,
        out_shape=jax.ShapeDtypeStruct((8, 2 * RANK, width), F32),
        compiler_params=params(16),
        cost_estimate=pl.CostEstimate(
            flops=2 * 8 * rows * 2 * half * 256, bytes_accessed=MIB, transcendentals=0
        ),
        name="down_grads",
    )(jnp.concatenate([idx[:8], slot_of]), back, *blocks)


def pack_kernel(slot, a0, a1, a2, a3, gbq, v0, v1, out):
    n = out.shape[0]
    down = a0[...] + a1[...].astype(F32) + a2[...].astype(F32) + a3[...].astype(F32)
    gbv = v0[...] + v1[...]
    wide = out.shape[2]
    for i in range(n):
        for j in range(n):

            @pl.when(slot[i] == j)
            def _():
                cols = slice(j * wide, (j + 1) * wide)
                out[i, : 2 * RANK, :] = down[:, cols]
                out[i, 2 * RANK : 3 * RANK, :] = gbq[:, cols]
                out[i, 3 * RANK : 3 * RANK + 8, :] = gbv[:, cols]
                out[i, 3 * RANK + 8 :, :] = jnp.zeros((8, wide), F32)


def pack(slot, pieces, gbq, v0, v1):
    n = slot.shape[0]
    return pl.pallas_call(
        pack_kernel,
        in_specs=[SM] + [VM] * 7,
        out_specs=VM,
        out_shape=jax.ShapeDtypeStruct((n, 3 * RANK + 16, gbq.shape[1] // n), F32),
        compiler_params=params(16),
        name="pack",
    )(slot, *pieces, gbq, v0, v1)


def unpack_kernel(n, counts, info, *refs):
    ins, (gaq, gav, gbq, gbv) = refs[:-4], refs[-4:]
    size = 3 * RANK + 16
    places = []
    for b, count in enumerate(counts):
        places += [b] * count
    seen = [0] * len(counts)
    for ref, b in zip(ins, places):
        seq = info[b]
        wide = ref.shape[1]
        for row in range(0, ref.shape[0], size):
            source = info[8 + seen[b]]
            seen[b] += 1
            part = ref[row : row + size, :].astype(F32)
            cols = pl.ds(pl.multiple_of(seq * (n * wide) + source * wide, wide), wide)
            gaq[:, cols] = part[:RANK]
            gav[:, cols] = part[RANK : 2 * RANK]
            gbq[:, cols] = part[2 * RANK : 3 * RANK]
            if b % 2 == 0:
                at = pl.ds(pl.multiple_of((seq // 2) * HEAD, HEAD), HEAD)
                for j in range(wide // HEAD):
                    first = (source * (wide // HEAD) + j) * 8
                    gbv[pl.ds(pl.multiple_of(first, 8), 8), at] = part[
                        3 * RANK : 3 * RANK + 8, j * HEAD : (j + 1) * HEAD
                    ]


def unpack(info, groups, n, model):
    counts = tuple(len(g) for g in groups)
    pieces = [v for g in groups for v in g]
    return pl.pallas_call(
        functools.partial(unpack_kernel, n, counts),
        in_specs=[SM] + [VM] * len(pieces),
        out_specs=[VM] * 4,
        out_shape=[
            jax.ShapeDtypeStruct((RANK, model), F32),
            jax.ShapeDtypeStruct((RANK, model), F32),
            jax.ShapeDtypeStruct((RANK, model), F32),
            jax.ShapeDtypeStruct((RANK, KV_HEADS * HEAD), F32),
        ],
        compiler_params=params(16),
        name="unpack",
    )(info, *pieces)


def shift(value, axis, by):
    n = lax.axis_size(axis)
    return lax.ppermute(value, axis, [(i, (i + by) % n) for i in range(n)])


def shards(
    rollouts,
    plan,
    lengths,
    rewards,
    output_gradient,
    query_projection,
    key_projection,
    value_projection,
    adapter_down_query,
    adapter_up_query,
    adapter_down_value,
    adapter_up_value,
):
    nz, nx = lax.axis_size("z"), lax.axis_size("x")
    z, x = lax.axis_index("z"), lax.axis_index("x")
    y, core = lax.axis_index("y"), lax.axis_index("core")
    seq = 2 * y + core
    total = output_gradient.shape[0]
    rows, model = rollouts.shape
    piece = rows // (nz * nx)
    swap = lambda v: lax.ppermute(v, "core", [(0, 1), (1, 0)])

    ys = [(y + d) % 4 for d in (0, 3, 1, 2)]
    idx = jnp.stack([2 * a + b for a in ys for b in (core, 1 - core)]).astype(jnp.int32)

    folded = fold(rollouts, piece).reshape(nz * nx, 2 * piece, model // 2)
    arrived = lax.all_to_all(folded, ("z", "x"), split_axis=0, concat_axis=0, tiled=True)
    order = lax.dynamic_slice_in_dim(plan, seq, 1, 0)
    own_l, own_r = order_rows(order, arrived.reshape(2 * rows, model // 2), piece)

    take = lambda w: lax.dynamic_slice_in_dim(w, y * HEAD, HEAD, 1)
    mine = jnp.where(core == 0, take(key_projection), take(value_projection))
    if nz == 8:
        three = jnp.concatenate([shift(mine, "z", 1), mine, shift(mine, "z", -1)], axis=0)
        low_z, high_z = shift(three, "z", 3), shift(three[: 2 * mine.shape[0]], "z", -3)
        over_z = jnp.concatenate([low_z, three, high_z], axis=0)
        zs = [(z + d) % nz for d in range(-4, 4)]
    else:
        over_z = jnp.concatenate([mine] + [shift(mine, "z", i) for i in range(1, nz)], axis=0)
        zs = [(z - i) % nz for i in range(nz)]
    over_x = jnp.concatenate([over_z] + [shift(over_z, "x", i) for i in range(1, nx)], axis=0)
    xs = [(x - i) % nx for i in range(nx)]
    per = model // (nz * nx * HEAD)
    into = [(b * nx + a) * per + i for a in xs for b in zs for i in range(per)]
    weights = join_weights(jnp.stack([core] + into).astype(jnp.int32), over_x, swap(over_x))
    up_value = take(adapter_up_value)
    down_both = jnp.concatenate([adapter_down_query.T, adapter_down_value.T], axis=0)

    ends = jnp.cumsum(lengths[0])
    starts = ends - lengths[0]
    places = jnp.arange(total, dtype=jnp.int32)
    segment = jnp.sum((places[:, None] >= ends[None, :]).astype(jnp.int32), axis=1)
    onehot = segment[:, None] == jnp.arange(lengths.shape[1], dtype=jnp.int32)[None, :]
    positions = places - jnp.sum(jnp.where(onehot, starts[None, :], 0), axis=1)
    column = jnp.arange(HEAD, dtype=jnp.int32)
    inv_freq = jnp.exp((column // 2).astype(F32) * (-2.0 * math.log(ROPE_BASE) / HEAD))
    angles = positions[:, None].astype(F32) * inv_freq[None, :]
    cos = jnp.cos(angles)
    ssin = jnp.where(column % 2 == 0, F32(-1.0), F32(1.0))[None, :] * jnp.sin(angles)
    advantage = rewards[0] - jnp.mean(rewards[0])
    adv_rows = jnp.sum(jnp.where(onehot, advantage[None, :], 0.0), axis=1)
    cot = (output_gradient.astype(F32) * adv_rows[:, None]).astype(BF)

    up_l, down_r = shift(own_l, "y", 1), shift(own_r, "y", -1)
    up_r, down_l = shift(own_r, "y", 1), shift(own_l, "y", -1)
    far_l, far_r = shift(up_l, "y", 1), shift(down_r, "y", -1)
    blocks, qs, lows = [], [], []
    for p, (l, r) in enumerate([(own_l, own_r), (up_l, up_r), (down_l, down_r), (far_l, far_r)]):
        four = (l, r, swap(l), swap(r))
        blocks += four
        q, low = project_q(
            p, idx, *four, query_projection, down_both, adapter_up_query, cos, ssin
        )
        qs.append(q)
        lows.append(low)
    k, v = project_kv(idx, blocks, weights, lows, up_value, cos, ssin)
    back, gbq, gbv = attention(
        idx, lengths, qs, lows, k, v, cot, cos, ssin, adapter_up_query, up_value
    )

    slot_of = [(j % 2 ^ core) * 4 + (j // 2 - y) % 4 for j in range(8)]
    down = down_grads(idx, jnp.stack(slot_of).astype(jnp.int32), back, blocks)
    gbv_other = swap(gbv)
    down = down[:4] + swap(down[4:])
    pieces = [down[0]] + [shift(down[b].astype(BF), "y", b) for b in (1, 2, 3)]
    xs = [(x + i) % nx for i in range(nx)]
    packed = pack(jnp.stack(xs).astype(jnp.int32), pieces, gbq, gbv, gbv_other)
    part = packed[0]
    for i in range(1, nx):
        part = part + shift(packed[i], "x", i)
    bit = 1
    while bit < nz:
        part = part + lax.ppermute(part, "z", [(i, i ^ bit) for i in range(nz)])
        bit *= 2
    full = part.astype(BF)
    mine = jnp.concatenate([full] + [shift(full, "x", i) for i in range(1, nx)], axis=0)
    ups, downs = shift(mine, "y", 1), shift(mine, "y", -1)
    cut = mine.shape[0] // 2
    far = [shift(ups[:cut], "y", 1), shift(downs[cut:], "y", -1)]
    groups = []
    for group in ([mine], [ups], [downs], far):
        groups += [group, [swap(v) for v in group]]
    info = jnp.stack([idx[b] for b in range(8)] + [(x - i) % nx for i in range(nx)])
    gaq, gav, gbq, gbv = unpack(info.astype(jnp.int32), groups, nx, model)
    return gaq.T, gav.T, gbq, gbv


def solution(mesh):
    groups, _ = mesh.devices.shape
    nx = 4 if groups % 4 == 0 else groups
    grid = Mesh(mesh.devices.reshape(groups // nx, nx, 4, 2), ("z", "x", "y", "core"))
    group, seq = ("z", "x"), ("y", "core")
    in_specs = (
        P(group + seq, None),
        P(group, None),
        P(group, None),
        P(group, None),
        P(group, seq),
        P(None, seq),
        P(group, None),
        P(group, None),
        P(),
        P(None, seq),
        P(),
        P(),
    )
    return jax.shard_map(
        shards, mesh=grid, in_specs=in_specs, out_specs=(P(), P(), P(), P()), check_vma=False
    )
```

```python
import functools
import math

import jax
import jax.numpy as jnp
from jax import lax
from jax.experimental import pallas as pl
from jax.experimental.pallas import tpu as pltpu
from jax.sharding import Mesh
from jax.sharding import PartitionSpec as P

HEAD = 128
KV_HEADS = 4
RANK = 32
ROPE_BASE = 500000.0
ADAPTER_SCALE = 2.0
LOG2E = math.log2(math.e)
BF = jnp.bfloat16
F32 = jnp.float32
MIB = 1 << 20


def mm(a, b, ca=1, cb=0):
    return lax.dot_general(a, b, (((ca,), (cb,)), ((), ())), preferred_element_type=F32)


def rope(u, cos, ssin, sign):
    even = lax.broadcasted_iota(jnp.int32, u.shape, 1) % 2 == 0
    swapped = jnp.where(even, pltpu.roll(u, HEAD - 1, 1), pltpu.roll(u, 1, 1))
    if sign > 0:
        return u * cos + ssin * swapped
    return u * cos - ssin * swapped


def params(mib):
    return pltpu.CompilerParams(vmem_limit_bytes=mib * MIB)


VM = pl.BlockSpec(memory_space=pltpu.VMEM)
SM = pl.BlockSpec(memory_space=pltpu.SMEM)


def fold_kernel(piece, x, out):
    rows, half = x.shape[0], x.shape[1] // 2
    r = lax.broadcasted_iota(jnp.int32, (2 * rows, 2 * rows), 0)
    c = lax.broadcasted_iota(jnp.int32, (2 * rows, 2 * rows), 1)
    inside = r % (2 * piece)
    source = (r // (2 * piece)) * piece + inside % piece + jnp.where(inside >= piece, rows, 0)
    pick = (source == c).astype(F32).astype(BF)
    both = jnp.concatenate([x[:, :half], x[:, half:]], axis=0)
    out[...] = mm(pick, both).astype(BF)


def fold(x, piece):
    rows, model = x.shape
    return pl.pallas_call(
        functools.partial(fold_kernel, piece),
        in_specs=[VM],
        out_specs=VM,
        out_shape=jax.ShapeDtypeStruct((2 * rows, model // 2), BF),
        compiler_params=params(16),
        name="fold",
    )(x)


def order_kernel(piece, plan, x, left, right):
    rows = left.shape[0]
    want = plan[...]
    want = (want // piece) * (2 * piece) + want % piece
    r = lax.broadcasted_iota(jnp.int32, (2 * rows, rows), 0)
    pick_l = (r == want).astype(F32).astype(BF)
    pick_r = (r == want + piece).astype(F32).astype(BF)
    left[...] = mm(pick_l, x[...], 0, 0).astype(BF)
    right[...] = mm(pick_r, x[...], 0, 0).astype(BF)


def order_rows(plan, x, piece):
    rows, half = x.shape[0] // 2, x.shape[1]
    return pl.pallas_call(
        functools.partial(order_kernel, piece),
        in_specs=[VM, VM],
        out_specs=[VM, VM],
        out_shape=[jax.ShapeDtypeStruct((rows, half), BF)] * 2,
        compiler_params=params(16),
        name="order_rows",
    )(plan, x)


def main_kernel(idx, into, lens, *refs):
    hs, (wq, wa, wb, dt, upq, upv, cos, ssin, cot_ref) = refs[:16], refs[16:25]
    own_out, send_out, gbq_out = refs[25:28]
    h_s, wq_s, wkv_s, q_s, k_s, v_s, low_s, qg_s, dv_s, h_sem, w_sem, kv_sem = refs[28:]
    total, model = h_s.shape
    half = model // 2
    rows = total // 8
    width = q_s.shape[1]
    core = idx[8]

    def block_copy(source, seq, side):
        at = pl.ds(pl.multiple_of(seq * rows, rows), rows)
        to = h_s.at[at, side * half : (side + 1) * half]
        return pltpu.make_async_copy(source, to, h_sem.at[2 * seq + side])

    wq_copy = pltpu.make_async_copy(wq, wq_s, w_sem)
    wq_copy.start()
    for b in range(8):
        for side in range(2):
            block_copy(hs[2 * b + side], idx[b], side).start()
    k_cols, v_cols = wkv_s.at[:, :HEAD], wkv_s.at[:, HEAD:]

    def weights(first, second):
        def block(i, carry):
            at = pl.ds(pl.multiple_of(i * HEAD, HEAD), HEAD)
            to = pl.ds(pl.multiple_of(into[i] * HEAD, HEAD), HEAD)
            pltpu.make_async_copy(first.at[at, :], wkv_s.at[to, :HEAD], kv_sem.at[0]).start()
            pltpu.make_async_copy(second.at[at, :], wkv_s.at[to, HEAD:], kv_sem.at[1]).start()
            return carry

        lax.fori_loop(0, model // HEAD, block, 0)

    pl.when(core == 0)(lambda: weights(wa, wb))
    pl.when(core != 0)(lambda: weights(wb, wa))
    dv_s[...] = jnp.zeros_like(dv_s)
    wq_copy.wait()
    for seq in range(8):
        for side in range(2):
            block_copy(hs[0], seq, side).wait()
    pltpu.make_async_copy(wa, k_cols, kv_sem.at[0]).wait()
    pltpu.make_async_copy(wb, v_cols, kv_sem.at[1]).wait()

    step = 4 * rows
    wide = 2 * HEAD

    def project(i, carry):
        at = pl.ds(pl.multiple_of(i * step, step), step)
        low = mm(h_s[at, :], dt[...], 1, 1).astype(BF)
        low_s[at, :] = low
        c, s = cos[at, :], ssin[at, :]
        for n in range(width // wide):
            cols = slice(n * wide, (n + 1) * wide)
            q = mm(h_s[at, :], wq_s[:, cols])
            q = q + ADAPTER_SCALE * mm(low[:, :RANK], upq[:, cols])
            for j in range(2):
                one = slice(n * wide + j * HEAD, n * wide + (j + 1) * HEAD)
                q_s[at, one] = rope(q[:, j * HEAD : (j + 1) * HEAD], c, s, 1).astype(BF)
        kv = mm(h_s[at, :], wkv_s[...])
        k_s[at, :] = rope(kv[:, :HEAD], c, s, 1).astype(BF)
        v = kv[:, HEAD:] + ADAPTER_SCALE * mm(low[:, RANK:], upv[...])
        v_s[at, :] = v.astype(BF)
        return carry

    lax.fori_loop(0, total // step, project, 0)

    scale = HEAD**-0.5
    blk = 2 * rows
    longest = 512
    ends = []
    end = jnp.int32(0)
    for n in range(lens.shape[1]):
        end = end + lens[0, n]
        ends.append(end)

    def head(h, carry):
        cols = pl.ds(pl.multiple_of(h * HEAD, HEAD), HEAD)
        for r in range(total // blk):
            lo, hi = max(0, r * blk - longest), (r + 1) * blk
            at = slice(r * blk, hi)
            keys = k_s[lo:hi, :]
            values = v_s[lo:hi, :]
            cot = cot_ref[at, cols]
            row = lax.broadcasted_iota(jnp.int32, (blk, 1), 0) + r * blk
            start = jnp.zeros((blk, 1), jnp.int32)
            for end in ends[:-1]:
                start = jnp.where(row >= end, end, start)
            col = lax.broadcasted_iota(jnp.int32, (blk, hi - lo), 1) + lo
            allowed = (col >= start) & (col <= row)
            s = mm(q_s[at, cols], keys, 1, 1) * (scale * LOG2E)
            s = jnp.where(allowed, s, -1e30)
            w = jnp.exp2(s - jnp.max(s, axis=1, keepdims=True))
            probs = w * (1.0 / jnp.sum(w, axis=1, keepdims=True))
            low = probs.astype(BF)
            dp = mm(cot, values, 1, 1)
            rowdot = jnp.sum(low.astype(F32) * dp, axis=1, keepdims=True)
            ds = (probs * (dp - rowdot) * scale).astype(BF)
            qg_s[at, cols] = rope(mm(ds, keys), cos[at, :], ssin[at, :], -1).astype(BF)
            dv_s[lo:hi, :] += mm(low, cot, 0, 0)
        return carry

    lax.fori_loop(0, width // HEAD, head, 0)

    qg = qg_s[...]
    vg = dv_s[...].astype(BF)
    low = low_s[...]
    gbq_out[...] = ADAPTER_SCALE * mm(low[:, :RANK], qg, 0, 0)
    gbv = ADAPTER_SCALE * mm(low[:, RANK:], vg, 0, 0)
    slot_rows = 2 * RANK
    for i in range(4):
        at = slice(4 * slot_rows, 4 * slot_rows + 8)
        part = gbv[8 * i : 8 * (i + 1), :]
        own_out[at, i * HEAD : (i + 1) * HEAD] = part
        send_out[at, i * HEAD : (i + 1) * HEAD] = part
    back_q = mm(upq[...], qg, 1, 1).astype(BF)
    back_v = mm(upv[...], vg, 1, 1).astype(BF)
    back = jnp.concatenate([back_q, back_v], axis=0)
    cut = model // 8
    for j in range(8):
        down = ADAPTER_SCALE * mm(back, h_s[:, j * cut : (j + 1) * cut])
        slot = pl.ds(pl.multiple_of(idx[9 + j] * slot_rows, slot_rows), slot_rows)

        @pl.when(core == j % 2)
        def _():
            own_out[slot, :] = down

        @pl.when(core != j % 2)
        def _():
            send_out[slot, :] = down


def device_gradients(idx, into, lengths, blocks, wq, wa, wb, dt, upq, upv, cos, ssin, cot):
    total, width = cot.shape
    model = wq.shape[0]
    any_ = pl.BlockSpec(memory_space=pl.ANY)
    slots = 8 * RANK + 8
    return pl.pallas_call(
        main_kernel,
        in_specs=[SM] * 3 + [any_] * 19 + [VM] * 6,
        out_specs=[VM] * 3,
        out_shape=[
            jax.ShapeDtypeStruct((slots, model // 8), F32),
            jax.ShapeDtypeStruct((slots, model // 8), F32),
            jax.ShapeDtypeStruct((RANK, width), F32),
        ],
        scratch_shapes=[
            pltpu.VMEM((total, model), BF),
            pltpu.VMEM((model, width), BF),
            pltpu.VMEM((model, 2 * HEAD), BF),
            pltpu.VMEM((total, width), BF),
            pltpu.VMEM((total, HEAD), BF),
            pltpu.VMEM((total, HEAD), BF),
            pltpu.VMEM((total, 2 * RANK), BF),
            pltpu.VMEM((total, width), BF),
            pltpu.VMEM((total, HEAD), F32),
            pltpu.SemaphoreType.DMA((16,)),
            pltpu.SemaphoreType.DMA,
            pltpu.SemaphoreType.DMA((2,)),
        ],
        compiler_params=params(40),
        cost_estimate=pl.CostEstimate(
            flops=25 * 10**9, bytes_accessed=16 * MIB, transcendentals=4 * 10**6
        ),
        name="device_gradients",
    )(idx, into, lengths, *blocks, wq, wa, wb, dt, upq, upv, cos, ssin, cot)


def pack_kernel(slot, own, a1, a2, a3, gbq, out):
    n = out.shape[0]
    down = own[: 2 * RANK, :]
    down = down + a1[...].astype(F32) + a2[...].astype(F32) + a3[...].astype(F32)
    gbv = own[8 * RANK :, :]
    wide = out.shape[2]
    for i in range(n):
        for j in range(n):

            @pl.when(slot[i] == j)
            def _():
                cols = slice(j * wide, (j + 1) * wide)
                out[i, : 2 * RANK, :] = down[:, cols]
                out[i, 2 * RANK : 3 * RANK, :] = gbq[:, cols]
                out[i, 3 * RANK : 3 * RANK + 8, :] = gbv[:, cols]
                out[i, 3 * RANK + 8 :, :] = jnp.zeros((8, wide), F32)


def pack(slot, own, pieces, gbq):
    n = slot.shape[0]
    return pl.pallas_call(
        pack_kernel,
        in_specs=[SM] + [VM] * 5,
        out_specs=VM,
        out_shape=jax.ShapeDtypeStruct((n, 3 * RANK + 16, gbq.shape[1] // n), F32),
        compiler_params=params(16),
        name="pack",
    )(slot, own, *pieces, gbq)


def unpack_kernel(n, counts, info, *refs):
    ins, (gaq, gav, gbq, gbv) = refs[:-4], refs[-4:]
    size = 3 * RANK + 16
    places = []
    for b, count in enumerate(counts):
        places += [b] * count
    seen = [0] * len(counts)
    for ref, b in zip(ins, places):
        seq = info[b]
        wide = ref.shape[1]
        for row in range(0, ref.shape[0], size):
            source = info[8 + seen[b]]
            seen[b] += 1
            part = ref[row : row + size, :].astype(F32)
            cols = pl.ds(pl.multiple_of(seq * (n * wide) + source * wide, wide), wide)
            gaq[:, cols] = part[:RANK]
            gav[:, cols] = part[RANK : 2 * RANK]
            gbq[:, cols] = part[2 * RANK : 3 * RANK]
            if b % 2 == 0:
                at = pl.ds(pl.multiple_of((seq // 2) * HEAD, HEAD), HEAD)
                for j in range(wide // HEAD):
                    first = (source * (wide // HEAD) + j) * 8
                    gbv[pl.ds(pl.multiple_of(first, 8), 8), at] = part[
                        3 * RANK : 3 * RANK + 8, j * HEAD : (j + 1) * HEAD
                    ]


def unpack(info, groups, n, model):
    counts = tuple(len(g) for g in groups)
    pieces = [v for g in groups for v in g]
    return pl.pallas_call(
        functools.partial(unpack_kernel, n, counts),
        in_specs=[SM] + [VM] * len(pieces),
        out_specs=[VM] * 4,
        out_shape=[
            jax.ShapeDtypeStruct((RANK, model), F32),
            jax.ShapeDtypeStruct((RANK, model), F32),
            jax.ShapeDtypeStruct((RANK, model), F32),
            jax.ShapeDtypeStruct((RANK, KV_HEADS * HEAD), F32),
        ],
        compiler_params=params(16),
        name="unpack",
    )(info, *pieces)


def shift(value, axis, by):
    n = lax.axis_size(axis)
    return lax.ppermute(value, axis, [(i, (i + by) % n) for i in range(n)])


def shards(
    rollouts,
    plan,
    lengths,
    rewards,
    output_gradient,
    query_projection,
    key_projection,
    value_projection,
    adapter_down_query,
    adapter_up_query,
    adapter_down_value,
    adapter_up_value,
):
    nz, nx = lax.axis_size("z"), lax.axis_size("x")
    z, x = lax.axis_index("z"), lax.axis_index("x")
    y, core = lax.axis_index("y"), lax.axis_index("core")
    seq = 2 * y + core
    total = output_gradient.shape[0]
    rows, model = rollouts.shape
    piece = rows // (nz * nx)
    swap = lambda v: lax.ppermute(v, "core", [(0, 1), (1, 0)])

    ys = [(y + d) % 4 for d in (0, 3, 1, 2)]
    idx = jnp.stack([2 * a + b for a in ys for b in (core, 1 - core)]).astype(jnp.int32)

    folded = fold(rollouts, piece).reshape(nz * nx, 2 * piece, model // 2)
    arrived = lax.all_to_all(folded, ("z", "x"), split_axis=0, concat_axis=0, tiled=True)
    order = lax.dynamic_slice_in_dim(plan, seq, 1, 0)

    ends = jnp.cumsum(lengths[0])
    starts = ends - lengths[0]
    places = jnp.arange(total, dtype=jnp.int32)
    segment = jnp.sum((places[:, None] >= ends[None, :]).astype(jnp.int32), axis=1)
    onehot = segment[:, None] == jnp.arange(lengths.shape[1], dtype=jnp.int32)[None, :]
    positions = places - jnp.sum(jnp.where(onehot, starts[None, :], 0), axis=1)
    column = jnp.arange(HEAD, dtype=jnp.int32)
    inv_freq = jnp.exp((column // 2).astype(F32) * (-2.0 * math.log(ROPE_BASE) / HEAD))
    angles = positions[:, None].astype(F32) * inv_freq[None, :]
    cos = jnp.cos(angles)
    ssin = jnp.where(column % 2 == 0, F32(-1.0), F32(1.0))[None, :] * jnp.sin(angles)
    advantage = rewards[0] - jnp.mean(rewards[0])
    adv_rows = jnp.sum(jnp.where(onehot, advantage[None, :], 0.0), axis=1)
    cot = (output_gradient.astype(F32) * adv_rows[:, None]).astype(BF)
    take = lambda w: lax.dynamic_slice_in_dim(w, y * HEAD, HEAD, 1)
    mine = jnp.where(core == 0, take(key_projection), take(value_projection))
    up_value = take(adapter_up_value)
    down_both = jnp.concatenate([adapter_down_query.T, adapter_down_value.T], axis=0)
    arrived, order, cos, ssin, cot, mine, up_value, down_both = lax.optimization_barrier(
        (arrived, order, cos, ssin, cot, mine, up_value, down_both)
    )

    own_l, own_r = order_rows(order, arrived.reshape(2 * rows, model // 2), piece)
    up_l, down_r = shift(own_l, "y", 1), shift(own_r, "y", -1)
    up_r, down_l = shift(own_r, "y", 1), shift(own_l, "y", -1)
    far_l, far_r = shift(up_l, "y", 1), shift(down_r, "y", -1)
    blocks = []
    for l, r in [(own_l, own_r), (up_l, up_r), (down_l, down_r), (far_l, far_r)]:
        blocks += [l, r, swap(l), swap(r)]

    mine, _ = lax.optimization_barrier((mine, own_l))
    if nz == 8:
        three = jnp.concatenate([shift(mine, "z", 1), mine, shift(mine, "z", -1)], axis=0)
        low_z, high_z = shift(three, "z", 3), shift(three[: 2 * mine.shape[0]], "z", -3)
        over_z = jnp.concatenate([low_z, three, high_z], axis=0)
        zs = [(z + d) % nz for d in range(-4, 4)]
    else:
        over_z = jnp.concatenate([mine] + [shift(mine, "z", i) for i in range(1, nz)], axis=0)
        zs = [(z - i) % nz for i in range(nz)]
    over_x = jnp.concatenate([over_z] + [shift(over_z, "x", i) for i in range(1, nx)], axis=0)
    xs = [(x - i) % nx for i in range(nx)]
    per = model // (nz * nx * HEAD)
    into = jnp.stack([(b * nx + a) * per + i for a in xs for b in zs for i in range(per)])

    slots = [(j // 2 - y) % 4 for j in range(8)]
    table = jnp.concatenate([idx, jnp.stack([core] + slots).astype(jnp.int32)])
    own, send, gbq = device_gradients(
        table,
        into.astype(jnp.int32),
        lengths,
        blocks,
        query_projection,
        over_x,
        swap(over_x),
        down_both,
        adapter_up_query,
        up_value,
        cos,
        ssin,
        cot,
    )

    own = own + swap(send)
    size = 2 * RANK
    pieces = [shift(own[size * b : size * (b + 1)].astype(BF), "y", b) for b in (1, 2, 3)]
    xs = [(x + i) % nx for i in range(nx)]
    packed = pack(jnp.stack(xs).astype(jnp.int32), own, pieces, gbq)
    part = packed[0]
    for i in range(1, nx):
        part = part + shift(packed[i], "x", i)
    pairs = lambda v, bit: lax.ppermute(v, "z", [(i, i ^ bit) for i in range(nz)])
    if nz >= 4:
        part = part + pairs(part, 1) + pairs(part, 2) + pairs(part, 3)
        bit = 4
    else:
        bit = 1
    while bit < nz:
        part = part + pairs(part, bit)
        bit *= 2
    full = part.astype(BF)
    mine = jnp.concatenate([full] + [shift(full, "x", i) for i in range(1, nx)], axis=0)
    ups, downs = shift(mine, "y", 1), shift(mine, "y", -1)
    cut = mine.shape[0] // 2
    far = [shift(ups[:cut], "y", 1), shift(downs[cut:], "y", -1)]
    groups = []
    for group in ([mine], [ups], [downs], far):
        groups += [group, [swap(v) for v in group]]
    info = jnp.stack([idx[b] for b in range(8)] + [(x - i) % nx for i in range(nx)])
    gaq, gav, gbq, gbv = unpack(info.astype(jnp.int32), groups, nx, model)
    return gaq.T, gav.T, gbq, gbv


def solution(mesh):
    groups, _ = mesh.devices.shape
    nx = 4 if groups % 4 == 0 else groups
    grid = Mesh(mesh.devices.reshape(groups // nx, nx, 4, 2), ("z", "x", "y", "core"))
    group, seq = ("z", "x"), ("y", "core")
    in_specs = (
        P(group + seq, None),
        P(group, None),
        P(group, None),
        P(group, None),
        P(group, seq),
        P(None, seq),
        P(group, None),
        P(group, None),
        P(),
        P(None, seq),
        P(),
        P(),
    )
    return jax.shard_map(
        shards, mesh=grid, in_specs=in_specs, out_specs=(P(), P(), P(), P()), check_vma=False
    )
```

```python
import functools
import math

import jax
import jax.numpy as jnp
from jax import lax
from jax.experimental import pallas as pl
from jax.experimental.pallas import tpu as pltpu
from jax.sharding import Mesh
from jax.sharding import PartitionSpec as P

HEAD = 128
KV_HEADS = 4
RANK = 32
ROPE_BASE = 500000.0
ADAPTER_SCALE = 2.0
LOG2E = math.log2(math.e)
BF = jnp.bfloat16
F32 = jnp.float32
MIB = 1 << 20


def mm(a, b, ca=1, cb=0):
    return lax.dot_general(a, b, (((ca,), (cb,)), ((), ())), preferred_element_type=F32)


def rope(u, cos, ssin, sign):
    even = lax.broadcasted_iota(jnp.int32, u.shape, 1) % 2 == 0
    swapped = jnp.where(even, pltpu.roll(u, HEAD - 1, 1), pltpu.roll(u, 1, 1))
    if sign > 0:
        return u * cos + ssin * swapped
    return u * cos - ssin * swapped


def params(mib):
    return pltpu.CompilerParams(vmem_limit_bytes=mib * MIB)


VM = pl.BlockSpec(memory_space=pltpu.VMEM)
SM = pl.BlockSpec(memory_space=pltpu.SMEM)


def fold_kernel(piece, x, out):
    rows, width = x.shape[0], out.shape[1]
    r = lax.broadcasted_iota(jnp.int32, (2 * rows, 2 * rows), 0)
    c = lax.broadcasted_iota(jnp.int32, (2 * rows, 2 * rows), 1)
    inside = r % (2 * piece)
    source = (r // (2 * piece)) * piece + inside % piece + jnp.where(inside >= piece, rows, 0)
    pick = (source == c).astype(F32).astype(BF)
    both = jnp.concatenate([x[:, :width], x[:, width:]], axis=0)
    out[...] = mm(pick, both).astype(BF)


def fold(x, piece):
    rows, model = x.shape
    return pl.pallas_call(
        functools.partial(fold_kernel, piece),
        in_specs=[VM],
        out_specs=VM,
        out_shape=jax.ShapeDtypeStruct((2 * rows, model // 2), BF),
        compiler_params=params(16),
        name="fold",
    )(x)


def order_kernel(piece, plan, x, left, right):
    rows = left.shape[0]
    want = plan[...]
    want = (want // piece) * (2 * piece) + want % piece
    r = lax.broadcasted_iota(jnp.int32, (2 * rows, rows), 0)
    pick_l = (r == want).astype(F32).astype(BF)
    pick_r = (r == want + piece).astype(F32).astype(BF)
    left[...] = mm(pick_l, x[...], 0, 0).astype(BF)
    right[...] = mm(pick_r, x[...], 0, 0).astype(BF)


def order_rows(plan, x, piece):
    rows, width = x.shape[0] // 2, x.shape[1]
    return pl.pallas_call(
        functools.partial(order_kernel, piece),
        in_specs=[VM, VM],
        out_specs=[VM, VM],
        out_shape=[jax.ShapeDtypeStruct((rows, width), BF)] * 2,
        compiler_params=params(16),
        name="order_rows",
    )(plan, x)


def main_kernel(places, idx, lens, *refs):
    hs, refs = refs[: len(places)], refs[len(places) :]
    wq, wa, wb, down_maps, cos_in, sin_in, cot_in, upq, upv = refs[:9]
    own_out, send_out, gbq_out = refs[9:12]
    h_s, wq_s, wkv_s, cos, ssin, cot_ref, q_s, k_s, v_s, low_s, qg_s, dv_s = refs[12:24]
    s_s, dp_s, p_s, ds_s = refs[24:26], refs[26:28], refs[28:30], refs[30:32]
    back_s, kt_s, vt_s, h_sem, w_sem, kv_sem = refs[32:]
    total, model = h_s.shape
    rows = total // 8
    width = q_s.shape[1]
    core = idx[8]

    copy = pltpu.make_async_copy
    k_cols, v_cols = wkv_s.at[:, :HEAD], wkv_s.at[:, HEAD : 2 * HEAD]

    def weights(first, second):
        copy(first, k_cols, kv_sem.at[0]).start()
        copy(second, v_cols, kv_sem.at[1]).start()

    small = [(down_maps, wkv_s.at[:, 2 * HEAD :]), (cos_in, cos), (sin_in, ssin), (cot_in, cot_ref)]
    late = [copy(a, b, w_sem.at[1 + i]) for i, (a, b) in enumerate(small)]
    blocks = []
    for n, (b, col) in enumerate(places):
        at = slice(b * rows, (b + 1) * rows)
        blocks.append(copy(hs[n], h_s.at[at, col : col + hs[n].shape[1]], h_sem.at[n]))
    first = [one for one, (b, _) in zip(blocks, places) if b < 4]
    second = [one for one, (b, _) in zip(blocks, places) if b >= 4]
    late[0].start()
    pl.when(core == 0)(lambda: weights(wa, wb))
    pl.when(core != 0)(lambda: weights(wb, wa))
    for one in first + late[1:3] + second:
        one.start()
    wq_copy = copy(wq, wq_s, w_sem.at[0])
    wq_copy.start()
    late[3].start()
    dv_s[...] = jnp.zeros_like(dv_s)

    step = 4 * rows
    wide = 2 * HEAD

    def spots(i):
        return [pl.ds(pl.multiple_of(idx[4 * i + j] * rows, rows), rows) for j in range(4)]

    def project_kv(i):
        kv = mm(h_s[i * step : (i + 1) * step, :], wkv_s[...])
        low = kv[:, 2 * HEAD : 2 * HEAD + 2 * RANK].astype(BF)
        v = kv[:, HEAD : 2 * HEAD] + ADAPTER_SCALE * mm(low[:, RANK:], upv[...])
        for j, at in enumerate(spots(i)):
            part = slice(j * rows, (j + 1) * rows)
            low_s[at, :] = low[part]
            k_s[at, :] = rope(kv[part, :HEAD], cos[at, :], ssin[at, :], 1).astype(BF)
            v_s[at, :] = v[part].astype(BF)

    def project_q(i, carry):
        ats = spots(i)
        low = jnp.concatenate([low_s[at, :RANK] for at in ats], axis=0)
        rows_i = pl.ds(pl.multiple_of(i * step, step), step)
        for n in range(width // wide):
            cols = slice(n * wide, (n + 1) * wide)
            q = mm(h_s[rows_i, :], wq_s[:, cols])
            q = q + ADAPTER_SCALE * mm(low, upq[:, cols])
            for j, at in enumerate(ats):
                part = q[j * rows : (j + 1) * rows]
                for h in range(2):
                    one = slice(n * wide + h * HEAD, n * wide + (h + 1) * HEAD)
                    turned = rope(part[:, h * HEAD : (h + 1) * HEAD], cos[at, :], ssin[at, :], 1)
                    q_s[at, one] = turned.astype(BF)
        return carry

    late[0].wait()
    copy(wa, k_cols, kv_sem.at[0]).wait()
    copy(wb, v_cols, kv_sem.at[1]).wait()
    for one in first + late[1:3]:
        one.wait()
    project_kv(0)
    for one in second:
        one.wait()
    project_kv(1)
    wq_copy.wait()
    lax.fori_loop(0, total // step, project_q, 0)
    late[3].wait()

    scale = HEAD**-0.5
    blk = 2 * rows
    longest = 512
    chunk = 32
    ends = []
    end = jnp.int32(0)
    for n in range(lens.shape[1]):
        end = end + lens[0, n]
        ends.append(end)

    kt_s[...] = k_s[...].T
    vt_s[...] = v_s[...].T
    blocks_n = total // blk
    lows = [max(0, r * blk - longest) for r in range(blocks_n)]

    def head(h, carry):
        cols = pl.ds(pl.multiple_of(h * HEAD, HEAD), HEAD)

        def ahead(r):
            lo, hi = lows[r], (r + 1) * blk
            at, buf = slice(r * blk, hi), r % 2
            for first in range(lo, hi, blk):
                some, to = slice(first, first + blk), slice(first - lo, first - lo + blk)

                def scores(some=some, to=to):
                    s_s[buf][:, to] = mm(q_s[at, cols], kt_s[:, some])

                def products(some=some, to=to):
                    dp_s[buf][:, to] = mm(cot_ref[at, cols], vt_s[:, some])

                yield scores
                yield products

        def elementwise(r):
            lo, hi = lows[r], (r + 1) * blk
            span, buf = slice(0, hi - lo), r % 2
            for first in range(0, blk, chunk):

                def piece(first=first):
                    some = slice(first, first + chunk)
                    row = lax.broadcasted_iota(jnp.int32, (chunk, 1), 0) + (r * blk + first)
                    start = jnp.zeros((chunk, 1), jnp.int32)
                    for end in ends[:-1]:
                        start = jnp.where(row >= end, end, start)
                    col = lax.broadcasted_iota(jnp.int32, (chunk, hi - lo), 1) + lo
                    s = s_s[buf][some, span] * (scale * LOG2E)
                    s = jnp.where((col >= start) & (col <= row), s, -1e30)
                    w = jnp.exp2(s - jnp.max(s, axis=1, keepdims=True))
                    probs = w * (1.0 / jnp.sum(w, axis=1, keepdims=True))
                    low = probs.astype(BF)
                    p_s[buf][some, span] = low
                    dp = dp_s[buf][some, span]
                    rowdot = jnp.sum(low.astype(F32) * dp, axis=1, keepdims=True)
                    ds_s[buf][some, span] = (probs * (dp - rowdot) * scale).astype(BF)

                yield piece

        def behind(r):
            lo, hi = lows[r], (r + 1) * blk
            at, buf = slice(r * blk, hi), r % 2

            def queries():
                dq = mm(ds_s[buf][:, : hi - lo], k_s[lo:hi, :])
                qg_s[at, cols] = rope(dq, cos[at, :], ssin[at, :], -1).astype(BF)

            yield queries
            for first in range(lo, hi, blk):

                def values(first=first):
                    some = slice(first - lo, first - lo + blk)
                    dv_s[first : first + blk, :] += mm(p_s[buf][:, some], cot_ref[at, cols], 0, 0)

                yield values

        for job in ahead(0):
            job()
        for r in range(blocks_n):
            jobs = list(behind(r - 1)) if r else []
            jobs += list(ahead(r + 1)) if r + 1 < blocks_n else []
            pieces = list(elementwise(r))
            done = 0
            for i, piece in enumerate(pieces):
                upto = len(jobs) * (i + 1) // len(pieces)
                for job in jobs[done:upto]:
                    job()
                done = upto
                piece()
        for job in behind(blocks_n - 1):
            job()
        return carry

    lax.fori_loop(0, width // HEAD, head, 0)

    qg = qg_s[...]
    vg = dv_s[...].astype(BF)
    low = low_s[...]
    gbq_out[...] = ADAPTER_SCALE * mm(low[:, :RANK], qg, 0, 0)
    gbv = ADAPTER_SCALE * mm(low[:, RANK:], vg, 0, 0)
    slot_rows = 2 * RANK
    for i in range(4):
        at = slice(4 * slot_rows, 4 * slot_rows + 8)
        part = gbv[8 * i : 8 * (i + 1), :]
        own_out[at, i * HEAD : (i + 1) * HEAD] = part
        send_out[at, i * HEAD : (i + 1) * HEAD] = part
    back_q = mm(upq[...], qg, 1, 1).astype(BF)
    back_v = mm(upv[...], vg, 1, 1).astype(BF)
    back_s[...] = jnp.concatenate([back_q, back_v], axis=0)
    parts = [back_s[:, pl.ds(pl.multiple_of(idx[b] * rows, rows), rows)] for b in range(8)]
    back = jnp.concatenate(parts, axis=1)
    cut = model // 8
    for j in range(8):
        down = ADAPTER_SCALE * mm(back, h_s[:, j * cut : (j + 1) * cut])
        slot = pl.ds(pl.multiple_of(idx[9 + j] * slot_rows, slot_rows), slot_rows)

        @pl.when(core == j % 2)
        def _():
            own_out[slot, :] = down

        @pl.when(core != j % 2)
        def _():
            send_out[slot, :] = down


def device_gradients(idx, lengths, blocks, wq, wa, wb, down_maps, cos, ssin, cot, upq, upv):
    total, width = cot.shape
    model = wq.shape[0]
    any_ = pl.BlockSpec(memory_space=pl.ANY)
    slots = 8 * RANK + 8
    places = tuple((b, col) for b, col, _ in blocks)
    window = (total // 4, total // 4 + 512)
    return pl.pallas_call(
        functools.partial(main_kernel, places),
        in_specs=[SM] * 2 + [any_] * (len(blocks) + 7) + [VM] * 2,
        out_specs=[VM] * 3,
        out_shape=[
            jax.ShapeDtypeStruct((slots, model // 8), F32),
            jax.ShapeDtypeStruct((slots, model // 8), F32),
            jax.ShapeDtypeStruct((RANK, width), F32),
        ],
        scratch_shapes=[
            pltpu.VMEM((total, model), BF),
            pltpu.VMEM((model, width), BF),
            pltpu.VMEM((model, 3 * HEAD), BF),
            pltpu.VMEM((total, HEAD), F32),
            pltpu.VMEM((total, HEAD), F32),
            pltpu.VMEM((total, width), BF),
            pltpu.VMEM((total, width), BF),
            pltpu.VMEM((total, HEAD), BF),
            pltpu.VMEM((total, HEAD), BF),
            pltpu.VMEM((total, 2 * RANK), BF),
            pltpu.VMEM((total, width), BF),
            pltpu.VMEM((total, HEAD), F32),
            *[pltpu.VMEM(window, F32)] * 4,
            *[pltpu.VMEM(window, BF)] * 4,
            pltpu.VMEM((2 * RANK, total), BF),
            pltpu.VMEM((HEAD, total), BF),
            pltpu.VMEM((HEAD, total), BF),
            pltpu.SemaphoreType.DMA((len(blocks),)),
            pltpu.SemaphoreType.DMA((5,)),
            pltpu.SemaphoreType.DMA((2,)),
        ],
        compiler_params=params(58),
        cost_estimate=pl.CostEstimate(
            flops=25 * 10**9, bytes_accessed=16 * MIB, transcendentals=4 * 10**6
        ),
        name="device_gradients",
    )(idx, lengths, *[v for _, _, v in blocks], wq, wa, wb, down_maps, cos, ssin, cot, upq, upv)


def pack_kernel(slot, own, a1, a2, a3, gbq, out):
    n = out.shape[0]
    down = own[: 2 * RANK, :]
    down = down + a1[...].astype(F32) + a2[...].astype(F32) + a3[...].astype(F32)
    gbv = own[8 * RANK :, :]
    wide = out.shape[2]
    for i in range(n):
        for j in range(n):

            @pl.when(slot[i] == j)
            def _():
                cols = slice(j * wide, (j + 1) * wide)
                out[i, : 2 * RANK, :] = down[:, cols].astype(BF)
                out[i, 2 * RANK : 3 * RANK, :] = gbq[:, cols].astype(BF)
                last = jnp.concatenate([gbv[:, cols], jnp.zeros((8, wide), F32)], axis=0)
                out[i, 3 * RANK :, :] = last.astype(BF)


def pack(slot, own, pieces, gbq):
    n = slot.shape[0]
    return pl.pallas_call(
        pack_kernel,
        in_specs=[SM] + [VM] * 5,
        out_specs=VM,
        out_shape=jax.ShapeDtypeStruct((n, 3 * RANK + 16, gbq.shape[1] // n), BF),
        compiler_params=params(16),
        name="pack",
    )(slot, own, *pieces, gbq)


def unpack_kernel(n, counts, info, *refs):
    ins, (gaq, gav, gbq, gbv) = refs[:-4], refs[-4:]
    size = 3 * RANK + 16
    places = []
    for b, count in enumerate(counts):
        places += [b] * count
    seen = [0] * len(counts)
    for ref, b in zip(ins, places):
        seq = info[b]
        wide = ref.shape[1]
        for row in range(0, ref.shape[0], size):
            source = info[8 + seen[b]]
            seen[b] += 1
            part = ref[row : row + size, :].astype(F32)
            cols = pl.ds(pl.multiple_of(seq * (n * wide) + source * wide, wide), wide)
            gaq[:, cols] = part[:RANK]
            gav[:, cols] = part[RANK : 2 * RANK]
            gbq[:, cols] = part[2 * RANK : 3 * RANK]
            if b % 2 == 0:
                at = pl.ds(pl.multiple_of((seq // 2) * HEAD, HEAD), HEAD)
                for j in range(wide // HEAD):
                    first = (source * (wide // HEAD) + j) * 8
                    gbv[pl.ds(pl.multiple_of(first, 8), 8), at] = part[
                        3 * RANK : 3 * RANK + 8, j * HEAD : (j + 1) * HEAD
                    ]


def unpack(info, groups, n, model):
    counts = tuple(len(g) for g in groups)
    pieces = [v for g in groups for v in g]
    return pl.pallas_call(
        functools.partial(unpack_kernel, n, counts),
        in_specs=[SM] + [VM] * len(pieces),
        out_specs=[VM] * 4,
        out_shape=[
            jax.ShapeDtypeStruct((RANK, model), F32),
            jax.ShapeDtypeStruct((RANK, model), F32),
            jax.ShapeDtypeStruct((RANK, model), F32),
            jax.ShapeDtypeStruct((RANK, KV_HEADS * HEAD), F32),
        ],
        compiler_params=params(16),
        name="unpack",
    )(info, *pieces)


def shift(value, axis, by):
    n = lax.axis_size(axis)
    return lax.ppermute(value, axis, [(i, (i + by) % n) for i in range(n)])


def shards(
    rollouts,
    plan,
    lengths,
    rewards,
    output_gradient,
    query_projection,
    key_projection,
    value_projection,
    adapter_down_query,
    adapter_up_query,
    adapter_down_value,
    adapter_up_value,
):
    nz, nx = lax.axis_size("z"), lax.axis_size("x")
    z, x = lax.axis_index("z"), lax.axis_index("x")
    y, core = lax.axis_index("y"), lax.axis_index("core")
    seq = 2 * y + core
    total = output_gradient.shape[0]
    rows, model = rollouts.shape
    piece = rows // (nz * nx)
    swap = lambda v: lax.ppermute(v, "core", [(0, 1), (1, 0)])

    ys = [(y + d) % 4 for d in (0, 3, 1, 2)]
    idx = jnp.stack([2 * a + b for a in ys for b in (core, 1 - core)]).astype(jnp.int32)

    take = lambda w: lax.dynamic_slice_in_dim(w, y * HEAD, HEAD, 1)
    mine = jnp.where(core == 0, take(key_projection), take(value_projection))
    gathered = lax.all_gather(mine, ("z", "x"), axis=0, tiled=True)

    rollouts, _ = lax.optimization_barrier((rollouts, mine))
    folded = fold(rollouts, piece).reshape(nz * nx, 2 * piece, model // 2)
    arrived = lax.all_to_all(folded, ("z", "x"), split_axis=0, concat_axis=0, tiled=True)
    order = lax.dynamic_slice_in_dim(plan, seq, 1, 0)

    ends = jnp.cumsum(lengths[0])
    starts = ends - lengths[0]
    places = jnp.arange(total, dtype=jnp.int32)
    segment = jnp.sum((places[:, None] >= ends[None, :]).astype(jnp.int32), axis=1)
    onehot = segment[:, None] == jnp.arange(lengths.shape[1], dtype=jnp.int32)[None, :]
    positions = places - jnp.sum(jnp.where(onehot, starts[None, :], 0), axis=1)
    column = jnp.arange(HEAD, dtype=jnp.int32)
    inv_freq = jnp.exp((column // 2).astype(F32) * (-2.0 * math.log(ROPE_BASE) / HEAD))
    angles = positions[:, None].astype(F32) * inv_freq[None, :]
    cos = jnp.cos(angles)
    ssin = jnp.where(column % 2 == 0, F32(-1.0), F32(1.0))[None, :] * jnp.sin(angles)
    advantage = rewards[0] - jnp.mean(rewards[0])
    adv_rows = jnp.sum(jnp.where(onehot, advantage[None, :], 0.0), axis=1)
    cot = (output_gradient.astype(F32) * adv_rows[:, None]).astype(BF)
    up_value = take(adapter_up_value)
    spare = jnp.zeros((model, HEAD - 2 * RANK), BF)
    down_maps = jnp.concatenate([adapter_down_query, adapter_down_value, spare], axis=1)
    slots = [(j // 2 - y) % 4 for j in range(8)]
    table = jnp.concatenate([idx, jnp.stack([core] + slots).astype(jnp.int32)])
    info = jnp.stack([idx[b] for b in range(8)] + [(x - i) % nx for i in range(nx)])
    info = info.astype(jnp.int32)
    xs = jnp.stack([(x + i) % nx for i in range(nx)]).astype(jnp.int32)
    arrived, order, cos, ssin, cot, up_value, down_maps, table, info, xs = (
        lax.optimization_barrier(
            (arrived, order, cos, ssin, cot, up_value, down_maps, table, info, xs)
        )
    )

    own_l, own_r = order_rows(order, arrived.reshape(2 * rows, model // 2), piece)
    up_l, down_r = shift(own_l, "y", 1), shift(own_r, "y", -1)
    up_r, down_l = shift(own_r, "y", 1), shift(own_l, "y", -1)
    far_l, far_r = shift(up_l, "y", 1), shift(down_r, "y", -1)
    far_l, far_r, gathered = lax.optimization_barrier((far_l, far_r, gathered))
    half = model // 2
    blocks = []
    for p, (l, r) in enumerate([(own_l, own_r), (up_l, up_r), (down_l, down_r), (far_l, far_r)]):
        for col, v in ((0, l), (half, r)):
            blocks += [(2 * p, col, v), (2 * p + 1, col, swap(v))]

    own, send, gbq = device_gradients(
        table,
        lengths,
        blocks,
        query_projection,
        gathered,
        swap(gathered),
        down_maps,
        cos,
        ssin,
        cot,
        adapter_up_query,
        up_value,
    )

    own = own + swap(send)
    size = 2 * RANK
    pieces = [shift(own[size * b : size * (b + 1)].astype(BF), "y", b) for b in (1, 2, 3)]
    packed = pack(xs, own, pieces, gbq)
    part = packed[0].astype(F32)
    for i in range(1, nx):
        part = part + shift(packed[i], "x", i).astype(F32)

    def from_pair(v, bits):
        return lax.ppermute(v, "z", [(i, i ^ bits) for i in range(nz)]).astype(F32)

    bits = 0
    if nz >= 4:
        sent = part.astype(BF)
        part = (sent.astype(F32) + from_pair(sent, 1)) + (from_pair(sent, 2) + from_pair(sent, 3))
        bits = 3
    while bits + 1 < nz:
        bits = 2 * bits + 1
        sent = part.astype(BF)
        part = sent.astype(F32) + from_pair(sent, bits)
    full = part.astype(BF)
    mine = jnp.concatenate([full] + [shift(full, "x", i) for i in range(1, nx)], axis=0)
    ups, downs = shift(mine, "y", 1), shift(mine, "y", -1)
    cut = mine.shape[0] // 2
    far = [shift(ups[:cut], "y", 1), shift(downs[cut:], "y", -1)]
    rest = [ups, downs, jnp.concatenate(far, axis=0)]
    moved = swap(jnp.concatenate(rest, axis=0))
    full_rows = mine.shape[0]
    groups = [[mine], [swap(mine)]]
    for i, v in enumerate(rest):
        groups += [[v], [moved[i * full_rows : (i + 1) * full_rows]]]
    gaq, gav, gbq, gbv = unpack(info, groups, nx, model)
    return gaq.T, gav.T, gbq, gbv


def solution(mesh):
    groups, _ = mesh.devices.shape
    nx = 4 if groups % 4 == 0 else groups
    grid = Mesh(mesh.devices.reshape(groups // nx, nx, 4, 2), ("z", "x", "y", "core"))
    group, seq = ("z", "x"), ("y", "core")
    in_specs = (
        P(group + seq, None),
        P(group, None),
        P(group, None),
        P(group, None),
        P(group, seq),
        P(None, seq),
        P(group, None),
        P(group, None),
        P(),
        P(None, seq),
        P(),
        P(),
    )
    return jax.shard_map(
        shards, mesh=grid, in_specs=in_specs, out_specs=(P(), P(), P(), P()), check_vma=False
    )
```

```python
import functools
import math

import jax
import jax.numpy as jnp
from jax import lax
from jax.experimental import pallas as pl
from jax.experimental.pallas import tpu as pltpu
from jax.sharding import Mesh
from jax.sharding import PartitionSpec as P

HEAD = 128
KV_HEADS = 4
RANK = 32
ROPE_BASE = 500000.0
ADAPTER_SCALE = 2.0
LOG2E = math.log2(math.e)
BF = jnp.bfloat16
F32 = jnp.float32
MIB = 1 << 20


def mm(a, b, ca=1, cb=0):
    return lax.dot_general(a, b, (((ca,), (cb,)), ((), ())), preferred_element_type=F32)


def rope(u, cos, ssin, sign):
    even = lax.broadcasted_iota(jnp.int32, u.shape, 1) % 2 == 0
    swapped = jnp.where(even, pltpu.roll(u, HEAD - 1, 1), pltpu.roll(u, 1, 1))
    if sign > 0:
        return u * cos + ssin * swapped
    return u * cos - ssin * swapped


def params(mib):
    return pltpu.CompilerParams(vmem_limit_bytes=mib * MIB)


VM = pl.BlockSpec(memory_space=pltpu.VMEM)
SM = pl.BlockSpec(memory_space=pltpu.SMEM)


def fold_kernel(piece, x, out):
    rows, width = x.shape[0], out.shape[1]
    r = lax.broadcasted_iota(jnp.int32, (2 * rows, 2 * rows), 0)
    c = lax.broadcasted_iota(jnp.int32, (2 * rows, 2 * rows), 1)
    inside = r % (2 * piece)
    source = (r // (2 * piece)) * piece + inside % piece + jnp.where(inside >= piece, rows, 0)
    pick = (source == c).astype(F32).astype(BF)
    both = jnp.concatenate([x[:, :width], x[:, width:]], axis=0)
    out[...] = mm(pick, both).astype(BF)


def fold(x, piece):
    rows, model = x.shape
    return pl.pallas_call(
        functools.partial(fold_kernel, piece),
        in_specs=[VM],
        out_specs=VM,
        out_shape=jax.ShapeDtypeStruct((2 * rows, model // 2), BF),
        compiler_params=params(16),
        name="fold",
    )(x)


def order_kernel(piece, plan, x, left, right):
    rows = left.shape[0]
    want = plan[...]
    want = (want // piece) * (2 * piece) + want % piece
    r = lax.broadcasted_iota(jnp.int32, (2 * rows, rows), 0)
    pick_l = (r == want).astype(F32).astype(BF)
    pick_r = (r == want + piece).astype(F32).astype(BF)
    left[...] = mm(pick_l, x[...], 0, 0).astype(BF)
    right[...] = mm(pick_r, x[...], 0, 0).astype(BF)


def order_rows(plan, x, piece):
    rows, width = x.shape[0] // 2, x.shape[1]
    return pl.pallas_call(
        functools.partial(order_kernel, piece),
        in_specs=[VM, VM],
        out_specs=[VM, VM],
        out_shape=[jax.ShapeDtypeStruct((rows, width), BF)] * 2,
        compiler_params=params(16),
        name="order_rows",
    )(plan, x)


def join_kernel(*refs):
    ins, out = refs[:-1], refs[-1]
    rows = ins[0].shape[0]
    for i, ref in enumerate(ins):
        out[i * rows : (i + 1) * rows, :] = ref[...]


def join(parts):
    rows, width = parts[0].shape
    return pl.pallas_call(
        join_kernel,
        in_specs=[VM] * len(parts),
        out_specs=VM,
        out_shape=jax.ShapeDtypeStruct((rows * len(parts), width), BF),
        compiler_params=params(16),
        name="join",
    )(*parts)


def main_kernel(places, pieces, idx, into, lens, *refs):
    hs, refs = refs[: len(places)], refs[len(places) :]
    was, wbs, refs = refs[:pieces], refs[pieces : 2 * pieces], refs[2 * pieces :]
    wq, down_maps, cos_in, sin_in, cot_in, upq, upv = refs[:7]
    refs = refs[7:]
    own_out, send_out, gbq_out = refs[:3]
    h_s, wq_s, wkv_s, cos, ssin, cot_ref, q_s, k_s, v_s, low_s, qg_s, dv_s = refs[3:15]
    s_s, dp_s, p_s, ds_s = refs[15:17], refs[17:19], refs[19:21], refs[21:23]
    back_s, kt_s, vt_s, h_sem, w_sem, kv_sem = refs[23:]
    total, model = h_s.shape
    rows = total // 8
    width = q_s.shape[1]
    core = idx[8]

    copy = pltpu.make_async_copy
    k_cols, v_cols = wkv_s.at[:, :HEAD], wkv_s.at[:, HEAD : 2 * HEAD]

    size = was[0].shape[0]

    def weights(firsts, seconds):
        for n in range(len(firsts)):

            def block(i, carry):
                at = pl.ds(pl.multiple_of(i * HEAD, HEAD), HEAD)
                place = into[n * (size // HEAD) + i]
                to = pl.ds(pl.multiple_of(place * HEAD, HEAD), HEAD)
                copy(firsts[n].at[at, :], wkv_s.at[to, :HEAD], kv_sem.at[0]).start()
                copy(seconds[n].at[at, :], wkv_s.at[to, HEAD : 2 * HEAD], kv_sem.at[1]).start()
                return carry

            lax.fori_loop(0, size // HEAD, block, 0)

    small = [(down_maps, wkv_s.at[:, 2 * HEAD :]), (cos_in, cos), (sin_in, ssin), (cot_in, cot_ref)]
    late = [copy(a, b, w_sem.at[1 + i]) for i, (a, b) in enumerate(small)]
    blocks = []
    for n, (b, col) in enumerate(places):
        at = slice(b * rows, (b + 1) * rows)
        blocks.append(copy(hs[n], h_s.at[at, col : col + hs[n].shape[1]], h_sem.at[n]))
    first = [one for one, (b, _) in zip(blocks, places) if b < 4]
    second = [one for one, (b, _) in zip(blocks, places) if b >= 4]
    late[0].start()
    pl.when(core == 0)(lambda: weights(was, wbs))
    pl.when(core != 0)(lambda: weights(wbs, was))
    for one in first + late[1:3] + second:
        one.start()
    wq_copy = copy(wq, wq_s, w_sem.at[0])
    wq_copy.start()
    late[3].start()
    dv_s[...] = jnp.zeros_like(dv_s)

    step = 4 * rows
    wide = 2 * HEAD

    def spots(i):
        return [pl.ds(pl.multiple_of(idx[4 * i + j] * rows, rows), rows) for j in range(4)]

    def project_kv(i):
        kv = mm(h_s[i * step : (i + 1) * step, :], wkv_s[...])
        low = kv[:, 2 * HEAD : 2 * HEAD + 2 * RANK].astype(BF)
        v = kv[:, HEAD : 2 * HEAD] + ADAPTER_SCALE * mm(low[:, RANK:], upv[...])
        for j, at in enumerate(spots(i)):
            part = slice(j * rows, (j + 1) * rows)
            low_s[at, :] = low[part]
            k_s[at, :] = rope(kv[part, :HEAD], cos[at, :], ssin[at, :], 1).astype(BF)
            v_s[at, :] = v[part].astype(BF)

    def project_q(i, carry):
        ats = spots(i)
        low = jnp.concatenate([low_s[at, :RANK] for at in ats], axis=0)
        rows_i = pl.ds(pl.multiple_of(i * step, step), step)
        for n in range(width // wide):
            cols = slice(n * wide, (n + 1) * wide)
            q = mm(h_s[rows_i, :], wq_s[:, cols])
            q = q + ADAPTER_SCALE * mm(low, upq[:, cols])
            for j, at in enumerate(ats):
                part = q[j * rows : (j + 1) * rows]
                for h in range(2):
                    one = slice(n * wide + h * HEAD, n * wide + (h + 1) * HEAD)
                    turned = rope(part[:, h * HEAD : (h + 1) * HEAD], cos[at, :], ssin[at, :], 1)
                    q_s[at, one] = turned.astype(BF)
        return carry

    late[0].wait()
    copy(down_maps, k_cols, kv_sem.at[0]).wait()
    copy(down_maps, v_cols, kv_sem.at[1]).wait()
    for one in first + late[1:3]:
        one.wait()
    project_kv(0)
    for one in second:
        one.wait()
    project_kv(1)
    wq_copy.wait()
    lax.fori_loop(0, total // step, project_q, 0)
    late[3].wait()

    scale = HEAD**-0.5
    blk = 2 * rows
    longest = 512
    chunk = 32
    ends = []
    end = jnp.int32(0)
    for n in range(lens.shape[1]):
        end = end + lens[0, n]
        ends.append(end)

    kt_s[...] = k_s[...].T
    vt_s[...] = v_s[...].T
    blocks_n = total // blk
    lows = [max(0, r * blk - longest) for r in range(blocks_n)]

    def head(h, carry):
        cols = pl.ds(pl.multiple_of(h * HEAD, HEAD), HEAD)

        def ahead(r):
            lo, hi = lows[r], (r + 1) * blk
            at, buf = slice(r * blk, hi), r % 2
            for first in range(lo, hi, blk):
                some, to = slice(first, first + blk), slice(first - lo, first - lo + blk)

                def scores(some=some, to=to):
                    s_s[buf][:, to] = mm(q_s[at, cols], kt_s[:, some])

                def products(some=some, to=to):
                    dp_s[buf][:, to] = mm(cot_ref[at, cols], vt_s[:, some])

                yield scores
                yield products

        def elementwise(r):
            lo, hi = lows[r], (r + 1) * blk
            span, buf = slice(0, hi - lo), r % 2
            for first in range(0, blk, chunk):

                def piece(first=first):
                    some = slice(first, first + chunk)
                    row = lax.broadcasted_iota(jnp.int32, (chunk, 1), 0) + (r * blk + first)
                    start = jnp.zeros((chunk, 1), jnp.int32)
                    for end in ends[:-1]:
                        start = jnp.where(row >= end, end, start)
                    col = lax.broadcasted_iota(jnp.int32, (chunk, hi - lo), 1) + lo
                    s = s_s[buf][some, span] * (scale * LOG2E)
                    s = jnp.where((col >= start) & (col <= row), s, -1e30)
                    w = jnp.exp2(s - jnp.max(s, axis=1, keepdims=True))
                    probs = w * (1.0 / jnp.sum(w, axis=1, keepdims=True))
                    low = probs.astype(BF)
                    p_s[buf][some, span] = low
                    dp = dp_s[buf][some, span]
                    rowdot = jnp.sum(low.astype(F32) * dp, axis=1, keepdims=True)
                    ds_s[buf][some, span] = (probs * (dp - rowdot) * scale).astype(BF)

                yield piece

        def behind(r):
            lo, hi = lows[r], (r + 1) * blk
            at, buf = slice(r * blk, hi), r % 2

            def queries():
                dq = mm(ds_s[buf][:, : hi - lo], k_s[lo:hi, :])
                qg_s[at, cols] = rope(dq, cos[at, :], ssin[at, :], -1).astype(BF)

            yield queries
            for first in range(lo, hi, blk):

                def values(first=first):
                    some = slice(first - lo, first - lo + blk)
                    dv_s[first : first + blk, :] += mm(p_s[buf][:, some], cot_ref[at, cols], 0, 0)

                yield values

        for job in ahead(0):
            job()
        for r in range(blocks_n):
            jobs = list(behind(r - 1)) if r else []
            jobs += list(ahead(r + 1)) if r + 1 < blocks_n else []
            pieces = list(elementwise(r))
            done = 0
            for i, piece in enumerate(pieces):
                upto = len(jobs) * (i + 1) // len(pieces)
                for job in jobs[done:upto]:
                    job()
                done = upto
                piece()
        for job in behind(blocks_n - 1):
            job()
        return carry

    lax.fori_loop(0, width // HEAD, head, 0)

    qg = qg_s[...]
    vg = dv_s[...].astype(BF)
    low = low_s[...]
    gbq_out[...] = ADAPTER_SCALE * mm(low[:, :RANK], qg, 0, 0)
    gbv = ADAPTER_SCALE * mm(low[:, RANK:], vg, 0, 0)
    slot_rows = 2 * RANK
    for i in range(4):
        at = slice(4 * slot_rows, 4 * slot_rows + 8)
        part = gbv[8 * i : 8 * (i + 1), :]
        own_out[at, i * HEAD : (i + 1) * HEAD] = part
        send_out[at, i * HEAD : (i + 1) * HEAD] = part
    back_q = mm(upq[...], qg, 1, 1).astype(BF)
    back_v = mm(upv[...], vg, 1, 1).astype(BF)
    back_s[...] = jnp.concatenate([back_q, back_v], axis=0)
    parts = [back_s[:, pl.ds(pl.multiple_of(idx[b] * rows, rows), rows)] for b in range(8)]
    back = jnp.concatenate(parts, axis=1)
    cut = model // 8
    for j in range(8):
        down = ADAPTER_SCALE * mm(back, h_s[:, j * cut : (j + 1) * cut])
        slot = pl.ds(pl.multiple_of(idx[9 + j] * slot_rows, slot_rows), slot_rows)

        @pl.when(core == j % 2)
        def _():
            own_out[slot, :] = down

        @pl.when(core != j % 2)
        def _():
            send_out[slot, :] = down


def device_gradients(
    idx, into, lengths, blocks, wq, was, wbs, down_maps, cos, ssin, cot, upq, upv
):
    total, width = cot.shape
    model = wq.shape[0]
    any_ = pl.BlockSpec(memory_space=pl.ANY)
    slots = 8 * RANK + 8
    places = tuple((b, col) for b, col, _ in blocks)
    window = (total // 4, total // 4 + 512)
    return pl.pallas_call(
        functools.partial(main_kernel, places, len(was)),
        in_specs=[SM] * 3 + [any_] * (len(blocks) + 2 * len(was) + 5) + [VM] * 2,
        out_specs=[VM] * 3,
        out_shape=[
            jax.ShapeDtypeStruct((slots, model // 8), F32),
            jax.ShapeDtypeStruct((slots, model // 8), F32),
            jax.ShapeDtypeStruct((RANK, width), F32),
        ],
        scratch_shapes=[
            pltpu.VMEM((total, model), BF),
            pltpu.VMEM((model, width), BF),
            pltpu.VMEM((model, 3 * HEAD), BF),
            pltpu.VMEM((total, HEAD), F32),
            pltpu.VMEM((total, HEAD), F32),
            pltpu.VMEM((total, width), BF),
            pltpu.VMEM((total, width), BF),
            pltpu.VMEM((total, HEAD), BF),
            pltpu.VMEM((total, HEAD), BF),
            pltpu.VMEM((total, 2 * RANK), BF),
            pltpu.VMEM((total, width), BF),
            pltpu.VMEM((total, HEAD), F32),
            *[pltpu.VMEM(window, F32)] * 4,
            *[pltpu.VMEM(window, BF)] * 4,
            pltpu.VMEM((2 * RANK, total), BF),
            pltpu.VMEM((HEAD, total), BF),
            pltpu.VMEM((HEAD, total), BF),
            pltpu.SemaphoreType.DMA((len(blocks),)),
            pltpu.SemaphoreType.DMA((5,)),
            pltpu.SemaphoreType.DMA((2,)),
        ],
        compiler_params=params(58),
        cost_estimate=pl.CostEstimate(
            flops=25 * 10**9, bytes_accessed=16 * MIB, transcendentals=4 * 10**6
        ),
        name="device_gradients",
    )(
        idx,
        into,
        lengths,
        *[v for _, _, v in blocks],
        *was,
        *wbs,
        wq,
        down_maps,
        cos,
        ssin,
        cot,
        upq,
        upv,
    )


def pack_kernel(slot, own, a1, a2, a3, gbq, out):
    n = out.shape[0]
    down = own[: 2 * RANK, :]
    down = down + a1[...].astype(F32) + a2[...].astype(F32) + a3[...].astype(F32)
    gbv = own[8 * RANK :, :]
    wide = out.shape[2]
    for i in range(n):
        for j in range(n):

            @pl.when(slot[i] == j)
            def _():
                cols = slice(j * wide, (j + 1) * wide)
                out[i, : 2 * RANK, :] = down[:, cols].astype(BF)
                out[i, 2 * RANK : 3 * RANK, :] = gbq[:, cols].astype(BF)
                last = jnp.concatenate([gbv[:, cols], jnp.zeros((8, wide), F32)], axis=0)
                out[i, 3 * RANK :, :] = last.astype(BF)


def pack(slot, own, pieces, gbq):
    n = slot.shape[0]
    return pl.pallas_call(
        pack_kernel,
        in_specs=[SM] + [VM] * 5,
        out_specs=VM,
        out_shape=jax.ShapeDtypeStruct((n, 3 * RANK + 16, gbq.shape[1] // n), BF),
        compiler_params=params(16),
        name="pack",
    )(slot, own, *pieces, gbq)


def unpack_kernel(n, counts, info, *refs):
    ins, (gaq, gav, gbq, gbv) = refs[:-4], refs[-4:]
    size = 3 * RANK + 16
    places = []
    for b, count in enumerate(counts):
        places += [b] * count
    seen = [0] * len(counts)
    for ref, b in zip(ins, places):
        seq = info[b]
        wide = ref.shape[1]
        for row in range(0, ref.shape[0], size):
            source = info[8 + seen[b]]
            seen[b] += 1
            part = ref[row : row + size, :].astype(F32)
            cols = pl.ds(pl.multiple_of(seq * (n * wide) + source * wide, wide), wide)
            gaq[:, cols] = part[:RANK]
            gav[:, cols] = part[RANK : 2 * RANK]
            gbq[:, cols] = part[2 * RANK : 3 * RANK]
            if b % 2 == 0:
                at = pl.ds(pl.multiple_of((seq // 2) * HEAD, HEAD), HEAD)
                for j in range(wide // HEAD):
                    first = (source * (wide // HEAD) + j) * 8
                    gbv[pl.ds(pl.multiple_of(first, 8), 8), at] = part[
                        3 * RANK : 3 * RANK + 8, j * HEAD : (j + 1) * HEAD
                    ]


def unpack(info, groups, n, model):
    counts = tuple(len(g) for g in groups)
    pieces = [v for g in groups for v in g]
    return pl.pallas_call(
        functools.partial(unpack_kernel, n, counts),
        in_specs=[SM] + [VM] * len(pieces),
        out_specs=[VM] * 4,
        out_shape=[
            jax.ShapeDtypeStruct((RANK, model), F32),
            jax.ShapeDtypeStruct((RANK, model), F32),
            jax.ShapeDtypeStruct((RANK, model), F32),
            jax.ShapeDtypeStruct((RANK, KV_HEADS * HEAD), F32),
        ],
        compiler_params=params(16),
        name="unpack",
    )(info, *pieces)


def shift(value, axis, by):
    n = lax.axis_size(axis)
    return lax.ppermute(value, axis, [(i, (i + by) % n) for i in range(n)])


def shards(
    rollouts,
    plan,
    lengths,
    rewards,
    output_gradient,
    query_projection,
    key_projection,
    value_projection,
    adapter_down_query,
    adapter_up_query,
    adapter_down_value,
    adapter_up_value,
):
    nz, nx = lax.axis_size("z"), lax.axis_size("x")
    z, x = lax.axis_index("z"), lax.axis_index("x")
    y, core = lax.axis_index("y"), lax.axis_index("core")
    seq = 2 * y + core
    total = output_gradient.shape[0]
    rows, model = rollouts.shape
    piece = rows // (nz * nx)
    swap = lambda v: lax.ppermute(v, "core", [(0, 1), (1, 0)])

    ys = [(y + d) % 4 for d in (0, 3, 1, 2)]
    idx = jnp.stack([2 * a + b for a in ys for b in (core, 1 - core)]).astype(jnp.int32)

    take = lambda w: lax.dynamic_slice_in_dim(w, y * HEAD, HEAD, 1)
    mine = jnp.where(core == 0, take(key_projection), take(value_projection))

    folded = fold(rollouts, piece).reshape(nz * nx, 2 * piece, model // 2)
    arrived = lax.all_to_all(folded, ("z", "x"), split_axis=0, concat_axis=0, tiled=True)
    order = lax.dynamic_slice_in_dim(plan, seq, 1, 0)

    ends = jnp.cumsum(lengths[0])
    starts = ends - lengths[0]
    places = jnp.arange(total, dtype=jnp.int32)
    segment = jnp.sum((places[:, None] >= ends[None, :]).astype(jnp.int32), axis=1)
    onehot = segment[:, None] == jnp.arange(lengths.shape[1], dtype=jnp.int32)[None, :]
    positions = places - jnp.sum(jnp.where(onehot, starts[None, :], 0), axis=1)
    column = jnp.arange(HEAD, dtype=jnp.int32)
    inv_freq = jnp.exp((column // 2).astype(F32) * (-2.0 * math.log(ROPE_BASE) / HEAD))
    angles = positions[:, None].astype(F32) * inv_freq[None, :]
    cos = jnp.cos(angles)
    ssin = jnp.where(column % 2 == 0, F32(-1.0), F32(1.0))[None, :] * jnp.sin(angles)
    advantage = rewards[0] - jnp.mean(rewards[0])
    adv_rows = jnp.sum(jnp.where(onehot, advantage[None, :], 0.0), axis=1)
    cot = (output_gradient.astype(F32) * adv_rows[:, None]).astype(BF)
    up_value = take(adapter_up_value)
    spare = jnp.zeros((model, HEAD - 2 * RANK), BF)
    down_maps = jnp.concatenate([adapter_down_query, adapter_down_value, spare], axis=1)
    slots = [(j // 2 - y) % 4 for j in range(8)]
    table = jnp.concatenate([idx, jnp.stack([core] + slots).astype(jnp.int32)])
    info = jnp.stack([idx[b] for b in range(8)] + [(x - i) % nx for i in range(nx)])
    info = info.astype(jnp.int32)
    xs = jnp.stack([(x + i) % nx for i in range(nx)]).astype(jnp.int32)
    over_z = [mine] + [shift(mine, "z", i) for i in range(1, nz)]
    zs, from_x = [(z - i) % nz for i in range(nz)], [(x - i) % nx for i in range(nx)]
    per = model // (nz * nx * HEAD)
    into = [(b * nx + a) * per + i for a in from_x for b in zs for i in range(per)]
    into = jnp.stack(into).astype(jnp.int32)
    early = (arrived, order, cos, ssin, cot, up_value, down_maps, table, info, xs, into, over_z)
    early = lax.optimization_barrier(early)
    arrived, order, cos, ssin, cot, up_value, down_maps, table, info, xs, into, over_z = early

    own_l, own_r = order_rows(order, arrived.reshape(2 * rows, model // 2), piece)
    up_l, down_r = shift(own_l, "y", 1), shift(own_r, "y", -1)
    far_l, far_r = shift(up_l, "y", 1), shift(down_r, "y", -1)
    last_l, last_r, _, _ = lax.optimization_barrier((own_l, own_r, far_l, far_r))
    up_r, down_l = shift(last_r, "y", 1), shift(last_l, "y", -1)
    over_z = lax.optimization_barrier((*over_z, up_l, down_r))[:-2]
    over_z = join(over_z)
    gathered = [over_z] + [shift(over_z, "x", i) for i in range(1, nx)]
    *gathered, up_r, down_l = lax.optimization_barrier((*gathered, up_r, down_l))
    half = model // 2
    blocks = []
    for p, (l, r) in enumerate([(own_l, own_r), (up_l, up_r), (down_l, down_r), (far_l, far_r)]):
        for col, v in ((0, l), (half, r)):
            blocks += [(2 * p, col, v), (2 * p + 1, col, swap(v))]

    own, send, gbq = device_gradients(
        table,
        into,
        lengths,
        blocks,
        query_projection,
        gathered,
        [swap(v) for v in gathered],
        down_maps,
        cos,
        ssin,
        cot,
        adapter_up_query,
        up_value,
    )

    own = own + swap(send)
    size = 2 * RANK
    pieces = [shift(own[size * b : size * (b + 1)].astype(BF), "y", b) for b in (1, 2, 3)]
    packed = pack(xs, own, pieces, gbq)
    part = packed[0].astype(F32)
    for i in range(1, nx):
        part = part + shift(packed[i], "x", i).astype(F32)

    def from_pair(v, bits):
        return lax.ppermute(v, "z", [(i, i ^ bits) for i in range(nz)]).astype(F32)

    bits = 0
    if nz >= 4:
        sent = part.astype(BF)
        part = (sent.astype(F32) + from_pair(sent, 1)) + (from_pair(sent, 2) + from_pair(sent, 3))
        bits = 3
    while bits + 1 < nz:
        bits = 2 * bits + 1
        sent = part.astype(BF)
        part = sent.astype(F32) + from_pair(sent, bits)
    full = part.astype(BF)
    mine = jnp.concatenate([full] + [shift(full, "x", i) for i in range(1, nx)], axis=0)
    ups, downs = shift(mine, "y", 1), shift(mine, "y", -1)
    cut = mine.shape[0] // 2
    far = [shift(ups[:cut], "y", 1), shift(downs[cut:], "y", -1)]
    rest = [ups, downs, jnp.concatenate(far, axis=0)]
    moved = swap(jnp.concatenate(rest, axis=0))
    full_rows = mine.shape[0]
    groups = [[mine], [swap(mine)]]
    for i, v in enumerate(rest):
        groups += [[v], [moved[i * full_rows : (i + 1) * full_rows]]]
    gaq, gav, gbq, gbv = unpack(info, groups, nx, model)
    return gaq.T, gav.T, gbq, gbv


def solution(mesh):
    groups, _ = mesh.devices.shape
    nx = 4 if groups % 4 == 0 else groups
    grid = Mesh(mesh.devices.reshape(groups // nx, nx, 4, 2), ("z", "x", "y", "core"))
    group, seq = ("z", "x"), ("y", "core")
    in_specs = (
        P(group + seq, None),
        P(group, None),
        P(group, None),
        P(group, None),
        P(group, seq),
        P(None, seq),
        P(group, None),
        P(group, None),
        P(),
        P(None, seq),
        P(),
        P(),
    )
    return jax.shard_map(
        shards, mesh=grid, in_specs=in_specs, out_specs=(P(), P(), P(), P()), check_vma=False
    )
```

```python
import functools
import math

import jax
import jax.numpy as jnp
from jax import lax
from jax.experimental import pallas as pl
from jax.experimental.pallas import tpu as pltpu
from jax.sharding import Mesh
from jax.sharding import PartitionSpec as P

HEAD = 128
KV_HEADS = 4
RANK = 32
ROPE_BASE = 500000.0
ADAPTER_SCALE = 2.0
LOG2E = math.log2(math.e)
BF = jnp.bfloat16
F32 = jnp.float32
MIB = 1 << 20


def mm(a, b, ca=1, cb=0):
    return lax.dot_general(a, b, (((ca,), (cb,)), ((), ())), preferred_element_type=F32)


def rope(u, cos, ssin, sign):
    even = lax.broadcasted_iota(jnp.int32, u.shape, 1) % 2 == 0
    swapped = jnp.where(even, pltpu.roll(u, HEAD - 1, 1), pltpu.roll(u, 1, 1))
    if sign > 0:
        return u * cos + ssin * swapped
    return u * cos - ssin * swapped


def params(mib):
    return pltpu.CompilerParams(vmem_limit_bytes=mib * MIB)


VM = pl.BlockSpec(memory_space=pltpu.VMEM)
SM = pl.BlockSpec(memory_space=pltpu.SMEM)


def fold_kernel(piece, x, out):
    rows, width = x.shape[0], out.shape[1]
    r = lax.broadcasted_iota(jnp.int32, (2 * rows, 2 * rows), 0)
    c = lax.broadcasted_iota(jnp.int32, (2 * rows, 2 * rows), 1)
    inside = r % (2 * piece)
    source = (r // (2 * piece)) * piece + inside % piece + jnp.where(inside >= piece, rows, 0)
    pick = (source == c).astype(F32).astype(BF)
    both = jnp.concatenate([x[:, :width], x[:, width:]], axis=0)
    out[...] = mm(pick, both).astype(BF)


def fold(x, piece):
    rows, model = x.shape
    return pl.pallas_call(
        functools.partial(fold_kernel, piece),
        in_specs=[VM],
        out_specs=VM,
        out_shape=jax.ShapeDtypeStruct((2 * rows, model // 2), BF),
        compiler_params=params(16),
        name="fold",
    )(x)


def order_kernel(piece, plan, x, left, right):
    rows = left.shape[0]
    want = plan[...]
    want = (want // piece) * (2 * piece) + want % piece
    r = lax.broadcasted_iota(jnp.int32, (2 * rows, rows), 0)
    pick_l = (r == want).astype(F32).astype(BF)
    pick_r = (r == want + piece).astype(F32).astype(BF)
    left[...] = mm(pick_l, x[...], 0, 0).astype(BF)
    right[...] = mm(pick_r, x[...], 0, 0).astype(BF)


def order_rows(plan, x, piece):
    rows, width = x.shape[0] // 2, x.shape[1]
    return pl.pallas_call(
        functools.partial(order_kernel, piece),
        in_specs=[VM, VM],
        out_specs=[VM, VM],
        out_shape=[jax.ShapeDtypeStruct((rows, width), BF)] * 2,
        compiler_params=params(16),
        name="order_rows",
    )(plan, x)


def join_kernel(*refs):
    ins, out = refs[:-1], refs[-1]
    row = 0
    for ref in ins:
        out[row : row + ref.shape[0], :] = ref[...]
        row += ref.shape[0]


def join(parts):
    rows, width = sum(v.shape[0] for v in parts), parts[0].shape[1]
    return pl.pallas_call(
        join_kernel,
        in_specs=[VM] * len(parts),
        out_specs=VM,
        out_shape=jax.ShapeDtypeStruct((rows, width), BF),
        compiler_params=params(16),
        name="join",
    )(*parts)


def main_kernel(places, pieces, idx, into, lens, *refs):
    hs, refs = refs[: len(places)], refs[len(places) :]
    was, wbs, refs = refs[:pieces], refs[pieces : 2 * pieces], refs[2 * pieces :]
    wq, down_maps, cos_in, sin_in, cot_in, upq, upv = refs[:7]
    refs = refs[7:]
    own_out, send_out, gbq_out = refs[:3]
    h_s, wq_s, wkv_s, cos, ssin, cot_ref, q_s, k_s, v_s, low_s, qg_s, dv_s = refs[3:15]
    s_s, dp_s, p_s, ds_s = refs[15:17], refs[17:19], refs[19:21], refs[21:23]
    back_s, kt_s, vt_s, h_sem, w_sem, kv_sem = refs[23:]
    total, model = h_s.shape
    rows = total // 8
    width = q_s.shape[1]
    core = idx[8]

    copy = pltpu.make_async_copy
    k_cols, v_cols = wkv_s.at[:, :HEAD], wkv_s.at[:, HEAD : 2 * HEAD]

    size = was[0].shape[0]

    def weights(firsts, seconds):
        for n in range(len(firsts)):

            def block(i, carry):
                at = pl.ds(pl.multiple_of(i * HEAD, HEAD), HEAD)
                place = into[n * (size // HEAD) + i]
                to = pl.ds(pl.multiple_of(place * HEAD, HEAD), HEAD)
                copy(firsts[n].at[at, :], wkv_s.at[to, :HEAD], kv_sem.at[0]).start()
                copy(seconds[n].at[at, :], wkv_s.at[to, HEAD : 2 * HEAD], kv_sem.at[1]).start()
                return carry

            lax.fori_loop(0, size // HEAD, block, 0)

    small = [(down_maps, wkv_s.at[:, 2 * HEAD :]), (cos_in, cos), (sin_in, ssin), (cot_in, cot_ref)]
    late = [copy(a, b, w_sem.at[1 + i]) for i, (a, b) in enumerate(small)]
    blocks = []
    for n, (b, col) in enumerate(places):
        at = slice(b * rows, (b + 1) * rows)
        blocks.append(copy(hs[n], h_s.at[at, col : col + hs[n].shape[1]], h_sem.at[n]))
    first = [one for one, (b, _) in zip(blocks, places) if b < 4]
    second = [one for one, (b, _) in zip(blocks, places) if b >= 4]
    late[0].start()
    pl.when(core == 0)(lambda: weights(was, wbs))
    pl.when(core != 0)(lambda: weights(wbs, was))
    for one in first + late[1:3] + second:
        one.start()
    wq_copy = copy(wq, wq_s, w_sem.at[0])
    wq_copy.start()
    late[3].start()
    dv_s[...] = jnp.zeros_like(dv_s)

    step = 4 * rows
    wide = 2 * HEAD

    def spots(i):
        return [pl.ds(pl.multiple_of(idx[4 * i + j] * rows, rows), rows) for j in range(4)]

    def project_kv(i):
        kv = mm(h_s[i * step : (i + 1) * step, :], wkv_s[...])
        low = kv[:, 2 * HEAD : 2 * HEAD + 2 * RANK].astype(BF)
        v = kv[:, HEAD : 2 * HEAD] + ADAPTER_SCALE * mm(low[:, RANK:], upv[...])
        for j, at in enumerate(spots(i)):
            part = slice(j * rows, (j + 1) * rows)
            low_s[at, :] = low[part]
            k_s[at, :] = rope(kv[part, :HEAD], cos[at, :], ssin[at, :], 1).astype(BF)
            v_s[at, :] = v[part].astype(BF)

    def project_q(i, carry):
        ats = spots(i)
        low = jnp.concatenate([low_s[at, :RANK] for at in ats], axis=0)
        rows_i = pl.ds(pl.multiple_of(i * step, step), step)
        for n in range(width // wide):
            cols = slice(n * wide, (n + 1) * wide)
            q = mm(h_s[rows_i, :], wq_s[:, cols])
            q = q + ADAPTER_SCALE * mm(low, upq[:, cols])
            for j, at in enumerate(ats):
                part = q[j * rows : (j + 1) * rows]
                for h in range(2):
                    one = slice(n * wide + h * HEAD, n * wide + (h + 1) * HEAD)
                    turned = rope(part[:, h * HEAD : (h + 1) * HEAD], cos[at, :], ssin[at, :], 1)
                    q_s[at, one] = turned.astype(BF)
        return carry

    late[0].wait()
    copy(down_maps, k_cols, kv_sem.at[0]).wait()
    copy(down_maps, v_cols, kv_sem.at[1]).wait()
    for one in first + late[1:3]:
        one.wait()
    project_kv(0)
    for one in second:
        one.wait()
    project_kv(1)
    wq_copy.wait()
    lax.fori_loop(0, total // step, project_q, 0)
    late[3].wait()

    scale = HEAD**-0.5
    blk = 2 * rows
    longest = 512
    chunk = 32
    ends = []
    end = jnp.int32(0)
    for n in range(lens.shape[1]):
        end = end + lens[0, n]
        ends.append(end)

    kt_s[...] = k_s[...].T
    vt_s[...] = v_s[...].T
    blocks_n = total // blk
    lows = [max(0, r * blk - longest) for r in range(blocks_n)]

    def head(h, carry):
        cols = pl.ds(pl.multiple_of(h * HEAD, HEAD), HEAD)

        def ahead(r):
            lo, hi = lows[r], (r + 1) * blk
            at, buf = slice(r * blk, hi), r % 2
            for first in range(lo, hi, blk):
                some, to = slice(first, first + blk), slice(first - lo, first - lo + blk)

                def scores(some=some, to=to):
                    s_s[buf][:, to] = mm(q_s[at, cols], kt_s[:, some])

                def products(some=some, to=to):
                    dp_s[buf][:, to] = mm(cot_ref[at, cols], vt_s[:, some])

                yield scores
                yield products

        def elementwise(r):
            lo, hi = lows[r], (r + 1) * blk
            span, buf = slice(0, hi - lo), r % 2
            for first in range(0, blk, chunk):

                def piece(first=first):
                    some = slice(first, first + chunk)
                    row = lax.broadcasted_iota(jnp.int32, (chunk, 1), 0) + (r * blk + first)
                    start = jnp.zeros((chunk, 1), jnp.int32)
                    for end in ends[:-1]:
                        start = jnp.where(row >= end, end, start)
                    col = lax.broadcasted_iota(jnp.int32, (chunk, hi - lo), 1) + lo
                    s = s_s[buf][some, span] * (scale * LOG2E)
                    s = jnp.where((col >= start) & (col <= row), s, -1e30)
                    w = jnp.exp2(s - jnp.max(s, axis=1, keepdims=True))
                    probs = w * (1.0 / jnp.sum(w, axis=1, keepdims=True))
                    low = probs.astype(BF)
                    p_s[buf][some, span] = low
                    dp = dp_s[buf][some, span]
                    rowdot = jnp.sum(low.astype(F32) * dp, axis=1, keepdims=True)
                    ds_s[buf][some, span] = (probs * (dp - rowdot) * scale).astype(BF)

                yield piece

        def behind(r):
            lo, hi = lows[r], (r + 1) * blk
            at, buf = slice(r * blk, hi), r % 2

            def queries():
                dq = mm(ds_s[buf][:, : hi - lo], k_s[lo:hi, :])
                qg_s[at, cols] = rope(dq, cos[at, :], ssin[at, :], -1).astype(BF)

            yield queries
            for first in range(lo, hi, blk):

                def values(first=first):
                    some = slice(first - lo, first - lo + blk)
                    dv_s[first : first + blk, :] += mm(p_s[buf][:, some], cot_ref[at, cols], 0, 0)

                yield values

        for job in ahead(0):
            job()
        for r in range(blocks_n):
            jobs = list(behind(r - 1)) if r else []
            jobs += list(ahead(r + 1)) if r + 1 < blocks_n else []
            pieces = list(elementwise(r))
            done = 0
            for i, piece in enumerate(pieces):
                upto = len(jobs) * (i + 1) // len(pieces)
                for job in jobs[done:upto]:
                    job()
                done = upto
                piece()
        for job in behind(blocks_n - 1):
            job()
        return carry

    lax.fori_loop(0, width // HEAD, head, 0)

    qg = qg_s[...]
    vg = dv_s[...].astype(BF)
    low = low_s[...]
    gbq_out[...] = ADAPTER_SCALE * mm(low[:, :RANK], qg, 0, 0)
    gbv = ADAPTER_SCALE * mm(low[:, RANK:], vg, 0, 0)
    slot_rows = 2 * RANK
    for i in range(4):
        at = slice(4 * slot_rows, 4 * slot_rows + 8)
        part = gbv[8 * i : 8 * (i + 1), :]
        own_out[at, i * HEAD : (i + 1) * HEAD] = part
        send_out[at, i * HEAD : (i + 1) * HEAD] = part
    back_q = mm(upq[...], qg, 1, 1).astype(BF)
    back_v = mm(upv[...], vg, 1, 1).astype(BF)
    back_s[...] = jnp.concatenate([back_q, back_v], axis=0)
    parts = [back_s[:, pl.ds(pl.multiple_of(idx[b] * rows, rows), rows)] for b in range(8)]
    back = jnp.concatenate(parts, axis=1)
    cut = model // 8
    for j in range(8):
        down = ADAPTER_SCALE * mm(back, h_s[:, j * cut : (j + 1) * cut])
        slot = pl.ds(pl.multiple_of(idx[9 + j] * slot_rows, slot_rows), slot_rows)

        @pl.when(core == j % 2)
        def _():
            own_out[slot, :] = down

        @pl.when(core != j % 2)
        def _():
            send_out[slot, :] = down


def device_gradients(
    idx, into, lengths, blocks, wq, was, wbs, down_maps, cos, ssin, cot, upq, upv
):
    total, width = cot.shape
    model = wq.shape[0]
    any_ = pl.BlockSpec(memory_space=pl.ANY)
    slots = 8 * RANK + 8
    places = tuple((b, col) for b, col, _ in blocks)
    window = (total // 4, total // 4 + 512)
    return pl.pallas_call(
        functools.partial(main_kernel, places, len(was)),
        in_specs=[SM] * 3 + [any_] * (len(blocks) + 2 * len(was) + 5) + [VM] * 2,
        out_specs=[VM] * 3,
        out_shape=[
            jax.ShapeDtypeStruct((slots, model // 8), F32),
            jax.ShapeDtypeStruct((slots, model // 8), F32),
            jax.ShapeDtypeStruct((RANK, width), F32),
        ],
        scratch_shapes=[
            pltpu.VMEM((total, model), BF),
            pltpu.VMEM((model, width), BF),
            pltpu.VMEM((model, 3 * HEAD), BF),
            pltpu.VMEM((total, HEAD), F32),
            pltpu.VMEM((total, HEAD), F32),
            pltpu.VMEM((total, width), BF),
            pltpu.VMEM((total, width), BF),
            pltpu.VMEM((total, HEAD), BF),
            pltpu.VMEM((total, HEAD), BF),
            pltpu.VMEM((total, 2 * RANK), BF),
            pltpu.VMEM((total, width), BF),
            pltpu.VMEM((total, HEAD), F32),
            *[pltpu.VMEM(window, F32)] * 4,
            *[pltpu.VMEM(window, BF)] * 4,
            pltpu.VMEM((2 * RANK, total), BF),
            pltpu.VMEM((HEAD, total), BF),
            pltpu.VMEM((HEAD, total), BF),
            pltpu.SemaphoreType.DMA((len(blocks),)),
            pltpu.SemaphoreType.DMA((5,)),
            pltpu.SemaphoreType.DMA((2,)),
        ],
        compiler_params=params(58),
        cost_estimate=pl.CostEstimate(
            flops=25 * 10**9, bytes_accessed=16 * MIB, transcendentals=4 * 10**6
        ),
        name="device_gradients",
    )(
        idx,
        into,
        lengths,
        *[v for _, _, v in blocks],
        *was,
        *wbs,
        wq,
        down_maps,
        cos,
        ssin,
        cot,
        upq,
        upv,
    )


def pack_kernel(slot, own, a1, a2, a3, gbq, out):
    n = out.shape[0]
    down = own[: 2 * RANK, :]
    down = down + a1[...].astype(F32) + a2[...].astype(F32) + a3[...].astype(F32)
    gbv = own[8 * RANK :, :]
    wide = out.shape[2]
    for i in range(n):
        for j in range(n):

            @pl.when(slot[i] == j)
            def _():
                cols = slice(j * wide, (j + 1) * wide)
                out[i, : 2 * RANK, :] = down[:, cols].astype(BF)
                out[i, 2 * RANK : 3 * RANK, :] = gbq[:, cols].astype(BF)
                last = jnp.concatenate([gbv[:, cols], jnp.zeros((8, wide), F32)], axis=0)
                out[i, 3 * RANK :, :] = last.astype(BF)


def pack(slot, own, pieces, gbq):
    n = slot.shape[0]
    return pl.pallas_call(
        pack_kernel,
        in_specs=[SM] + [VM] * 5,
        out_specs=VM,
        out_shape=jax.ShapeDtypeStruct((n, 3 * RANK + 16, gbq.shape[1] // n), BF),
        compiler_params=params(16),
        name="pack",
    )(slot, own, *pieces, gbq)


def unpack_kernel(n, counts, info, *refs):
    ins, (gaq, gav, gbq, gbv) = refs[:-4], refs[-4:]
    size = 3 * RANK + 16
    places = []
    for b, count in enumerate(counts):
        places += [b] * count
    seen = [0] * len(counts)
    for ref, b in zip(ins, places):
        seq = info[b]
        wide = ref.shape[1]
        for row in range(0, ref.shape[0], size):
            source = info[8 + seen[b]]
            seen[b] += 1
            part = ref[row : row + size, :].astype(F32)
            cols = pl.ds(pl.multiple_of(seq * (n * wide) + source * wide, wide), wide)
            gaq[:, cols] = part[:RANK]
            gav[:, cols] = part[RANK : 2 * RANK]
            gbq[:, cols] = part[2 * RANK : 3 * RANK]
            if b % 2 == 0:
                at = pl.ds(pl.multiple_of((seq // 2) * HEAD, HEAD), HEAD)
                for j in range(wide // HEAD):
                    first = (source * (wide // HEAD) + j) * 8
                    gbv[pl.ds(pl.multiple_of(first, 8), 8), at] = part[
                        3 * RANK : 3 * RANK + 8, j * HEAD : (j + 1) * HEAD
                    ]


def unpack(info, groups, n, model):
    counts = tuple(len(g) for g in groups)
    pieces = [v for g in groups for v in g]
    return pl.pallas_call(
        functools.partial(unpack_kernel, n, counts),
        in_specs=[SM] + [VM] * len(pieces),
        out_specs=[VM] * 4,
        out_shape=[
            jax.ShapeDtypeStruct((RANK, model), F32),
            jax.ShapeDtypeStruct((RANK, model), F32),
            jax.ShapeDtypeStruct((RANK, model), F32),
            jax.ShapeDtypeStruct((RANK, KV_HEADS * HEAD), F32),
        ],
        compiler_params=params(16),
        name="unpack",
    )(info, *pieces)


def shift(value, axis, by):
    n = lax.axis_size(axis)
    return lax.ppermute(value, axis, [(i, (i + by) % n) for i in range(n)])


def shards(
    rollouts,
    plan,
    lengths,
    rewards,
    output_gradient,
    query_projection,
    key_projection,
    value_projection,
    adapter_down_query,
    adapter_up_query,
    adapter_down_value,
    adapter_up_value,
):
    nz, nx = lax.axis_size("z"), lax.axis_size("x")
    z, x = lax.axis_index("z"), lax.axis_index("x")
    y, core = lax.axis_index("y"), lax.axis_index("core")
    seq = 2 * y + core
    total = output_gradient.shape[0]
    rows, model = rollouts.shape
    piece = rows // (nz * nx)
    swap = lambda v: lax.ppermute(v, "core", [(0, 1), (1, 0)])

    ys = [(y + d) % 4 for d in (0, 3, 1, 2)]
    idx = jnp.stack([2 * a + b for a in ys for b in (core, 1 - core)]).astype(jnp.int32)

    take = lambda w: lax.dynamic_slice_in_dim(w, y * HEAD, HEAD, 1)
    mine = jnp.where(core == 0, take(key_projection), take(value_projection))

    folded = fold(rollouts, piece).reshape(nz * nx, 2 * piece, model // 2)
    arrived = lax.all_to_all(folded, ("z", "x"), split_axis=0, concat_axis=0, tiled=True)
    order = lax.dynamic_slice_in_dim(plan, seq, 1, 0)

    ends = jnp.cumsum(lengths[0])
    starts = ends - lengths[0]
    places = jnp.arange(total, dtype=jnp.int32)
    segment = jnp.sum((places[:, None] >= ends[None, :]).astype(jnp.int32), axis=1)
    onehot = segment[:, None] == jnp.arange(lengths.shape[1], dtype=jnp.int32)[None, :]
    positions = places - jnp.sum(jnp.where(onehot, starts[None, :], 0), axis=1)
    column = jnp.arange(HEAD, dtype=jnp.int32)
    inv_freq = jnp.exp((column // 2).astype(F32) * (-2.0 * math.log(ROPE_BASE) / HEAD))
    angles = positions[:, None].astype(F32) * inv_freq[None, :]
    cos = jnp.cos(angles)
    ssin = jnp.where(column % 2 == 0, F32(-1.0), F32(1.0))[None, :] * jnp.sin(angles)
    advantage = rewards[0] - jnp.mean(rewards[0])
    adv_rows = jnp.sum(jnp.where(onehot, advantage[None, :], 0.0), axis=1)
    cot = (output_gradient.astype(F32) * adv_rows[:, None]).astype(BF)
    up_value = take(adapter_up_value)
    spare = jnp.zeros((model, HEAD - 2 * RANK), BF)
    down_maps = jnp.concatenate([adapter_down_query, adapter_down_value, spare], axis=1)
    slots = [(j // 2 - y) % 4 for j in range(8)]
    table = jnp.concatenate([idx, jnp.stack([core] + slots).astype(jnp.int32)])
    info = jnp.stack([idx[b] for b in range(8)] + [(x - i) % nx for i in range(nx)])
    info = info.astype(jnp.int32)
    xs = jnp.stack([(x + i) % nx for i in range(nx)]).astype(jnp.int32)
    from_x = [(x - i) % nx for i in range(nx)]
    if nz == 8:
        three = join([shift(mine, "z", 1), mine, shift(mine, "z", -1)])
        two = three[: 2 * mine.shape[0]]
        over_z = [shift(three, "z", 3), three, shift(two, "z", -3)]
        zs = [(z + d) % nz for d in range(-4, 4)]
    else:
        over_z = [mine] + [shift(mine, "z", i) for i in range(1, nz)]
        zs = [(z - i) % nz for i in range(nz)]
    per = model // (nz * nx * HEAD)
    into = [(b * nx + a) * per + i for a in from_x for b in zs for i in range(per)]
    into = jnp.stack(into).astype(jnp.int32)
    early = (arrived, order, cos, ssin, cot, up_value, down_maps, table, info, xs, into, over_z)
    early = lax.optimization_barrier(early)
    arrived, order, cos, ssin, cot, up_value, down_maps, table, info, xs, into, over_z = early

    own_l, own_r = order_rows(order, arrived.reshape(2 * rows, model // 2), piece)
    up_l, down_r = shift(own_l, "y", 1), shift(own_r, "y", -1)
    far_l, far_r = shift(up_l, "y", 1), shift(down_r, "y", -1)
    moved = [swap(v) for v in (own_l, own_r, up_l, down_r)]
    last_l, last_r, far_l, far_r, *moved = lax.optimization_barrier(
        (own_l, own_r, far_l, far_r, *moved)
    )
    up_r, down_l = shift(last_r, "y", 1), shift(last_l, "y", -1)
    over_z = lax.optimization_barrier((*over_z, up_l, down_r))[:-2]
    over_z = join(over_z)
    gathered = [over_z] + [shift(over_z, "x", i) for i in range(1, nx)]
    *gathered, up_r, down_l = lax.optimization_barrier((*gathered, up_r, down_l))
    half = model // 2
    blocks = []
    others = [*moved[:3], swap(up_r), swap(down_l), moved[3], swap(far_l), swap(far_r)]
    pairs_of = [own_l, own_r, up_l, up_r, down_l, down_r, far_l, far_r]
    for n, (v, other) in enumerate(zip(pairs_of, others)):
        b, col = n // 2 * 2, n % 2 * half
        blocks += [(b, col, v), (b + 1, col, other)]

    own, send, gbq = device_gradients(
        table,
        into,
        lengths,
        blocks,
        query_projection,
        gathered,
        [swap(v) for v in gathered],
        down_maps,
        cos,
        ssin,
        cot,
        adapter_up_query,
        up_value,
    )

    own = own + swap(send)
    size = 2 * RANK
    pieces = [shift(own[size * b : size * (b + 1)].astype(BF), "y", b) for b in (1, 2, 3)]
    packed = pack(xs, own, pieces, gbq)
    part = packed[0].astype(F32)
    for i in range(1, nx):
        part = part + shift(packed[i], "x", i).astype(F32)

    def from_pair(v, bits):
        return lax.ppermute(v, "z", [(i, i ^ bits) for i in range(nz)]).astype(F32)

    bits = 0
    if nz >= 4:
        sent = part.astype(BF)
        part = (sent.astype(F32) + from_pair(sent, 1)) + (from_pair(sent, 2) + from_pair(sent, 3))
        bits = 3
    while bits + 1 < nz:
        bits = 2 * bits + 1
        sent = part.astype(BF)
        part = sent.astype(F32) + from_pair(sent, bits)
    full = part.astype(BF)
    mine = jnp.concatenate([full] + [shift(full, "x", i) for i in range(1, nx)], axis=0)
    ups, downs = shift(mine, "y", 1), shift(mine, "y", -1)
    cut = mine.shape[0] // 2
    far = [shift(ups[:cut], "y", 1), shift(downs[cut:], "y", -1)]
    rest = [ups, downs, jnp.concatenate(far, axis=0)]
    moved = swap(jnp.concatenate(rest, axis=0))
    full_rows = mine.shape[0]
    groups = [[mine], [swap(mine)]]
    for i, v in enumerate(rest):
        groups += [[v], [moved[i * full_rows : (i + 1) * full_rows]]]
    gaq, gav, gbq, gbv = unpack(info, groups, nx, model)
    return gaq.T, gav.T, gbq, gbv


def solution(mesh):
    groups, _ = mesh.devices.shape
    nx = 4 if groups % 4 == 0 else groups
    grid = Mesh(mesh.devices.reshape(groups // nx, nx, 4, 2), ("z", "x", "y", "core"))
    group, seq = ("z", "x"), ("y", "core")
    in_specs = (
        P(group + seq, None),
        P(group, None),
        P(group, None),
        P(group, None),
        P(group, seq),
        P(None, seq),
        P(group, None),
        P(group, None),
        P(),
        P(None, seq),
        P(),
        P(),
    )
    return jax.shard_map(
        shards, mesh=grid, in_specs=in_specs, out_specs=(P(), P(), P(), P()), check_vma=False
    )
```
